256 devices in a mesh: tm: 32 (over y, z_hi, core), space: 8 (over x, z_lo).
Axes of the slice: x: 4, y: 4, z: 8 (z_hi: 4, z_lo: 2; z = z_hi * 2 + z_lo), core: 2. Of those that a mesh axis runs over, the one named last changes fastest.
Arguments:
- states: float32 [32, 64, 2048], P('tm', None, 'space'), may hold values from -6 to 6
- initial: float32 [64, 2048], P(None, 'space'), may hold values from -6 to 6
- source: float32 [128, 64, 2048], P('tm', None, 'space'), may hold values from -3 to 3
- mass: float32 [64, 2048], P(None, 'space'), may hold values from 0.85 to 1
- inv_fine: float32 [64, 64, 2048], P(None, None, 'space'), may hold values from -0.12 to 0.95, as said below
- inv_coarse: float32 [64, 64, 2048], P(None, None, 'space'), may hold values from -0.12 to 0.97, as said below
- face_mats: float32 [6, 16, 16], replicated, may hold values from -1.5 to 1.5
- face_coef: float32 [6, 2048], P(None, 'space'), may hold values from 0.05 to 0.4
- neighbours: int32 [6, 2048], P(None, 'space'), may hold values from 0 to 383, as said below
- rims: int32 [2, 512], P(None, 'space'), may hold values from 0 to 255, as said below
Outputs:
- c_points: float32 [32, 64, 2048], P('tm', None, 'space')
- f_points: float32 [96, 64, 2048], P('tm', None, 'space')
- c_residual: float32 [32, 64, 2048], P('tm', None, 'space')
The draws below stay inside these ranges and needn't reach their ends.
Inputs may be any that keep to these rules, and one draw needn't show every extreme that they name: On each device, neighbours[f, e] numbers the element across face f of its own element e: 0 to 255 an own element, 256 + j the j-th element of rims[1] of the device before along space (cyclically), 320 + j the j-th element of rims[0] of the device after. Every element has six neighbours and the relation is symmetric. The elements form 4 layers along the first direction: layer 0 is rims[0], the element across face 1 of the j-th element of layer l is the j-th element of layer l + 1, and layer 3 is rims[1] in order; across faces 0 and 1 of the j-th element of layers 0 and 3 lie the j-th rim elements of the devices before and after; across faces 2 to 5 lies an own element of the same layer. On each device, rims[0] and rims[1] each list 64 distinct own elements, numbered 0 to 255 on that device; the two lists are disjoint. On every device, element 0 is in rims[0] and element 256 - 1 in rims[1]. `inv_fine`: entries of the fine block inverses. `inv_coarse`: entries of the coarse block inverses.
All inputs are finite; a program needn't handle non-finite values.
Results may differ from the reference program's by a relative error of at most 0.0003.
Values sent between devices are 32-bit elements; how exact they have to be, the bound alone decides.
No kernel may reach another device: no remote copies, remote signals or barrier semaphores. Data moves between devices by JAX's collectives and lax.ppermute only.
A program may use at most 320 MiB of HBM per device.

```python
import math
import jax
import jax.numpy as jnp
from jax import lax

NODES = 64
FACE_NODES = 16
LX = 4
EY = 8
EZ = 8
STEP_SLICE = 4
E_DEV = 256
ELEMS = 2048
SLICES = 32
STEPS = 128
N_TM = 32
N_SPACE = 8


def pin_value(order, value, slot_id):
    held = order[slot_id]
    order = jnp.where(order == value, held, order)
    return order.at[slot_id].set(value)


def cell_positions(key):
    keys = jax.random.split(key, N_SPACE)

    def one_order(single):
        order = jax.random.permutation(single, E_DEV).astype(jnp.int32)
        order = pin_value(order, 0, 0)
        return pin_value(order, E_DEV - 1, E_DEV - 1)
    return jax.vmap(one_order)(keys)


def cell_number(xpos, ypos, zpos):
    return (xpos * EY + ypos) * EZ + zpos


def draw_neighbours(key, part):
    base_key = key
    positions = cell_positions(base_key)
    cells = jnp.arange(E_DEV, dtype=jnp.int32)
    xpos = cells // (EY * EZ)
    ypos = cells // EZ % EY
    zpos = cells % EZ
    rim_slot = ypos * EZ + zpos

    def one_device(where_cell):
        lower_x = jnp.where(xpos > 0, where_cell[cell_number((xpos - 1) % LX, ypos, zpos)], E_DEV + rim_slot)
        upper_x = jnp.where(xpos < LX - 1, where_cell[cell_number((xpos + 1) % LX, ypos, zpos)], E_DEV + EY * EZ + rim_slot)
        lower_y = where_cell[cell_number(xpos, (ypos - 1) % EY, zpos)]
        upper_y = where_cell[cell_number(xpos, (ypos + 1) % EY, zpos)]
        lower_z = where_cell[cell_number(xpos, ypos, (zpos - 1) % EZ)]
        upper_z = where_cell[cell_number(xpos, ypos, (zpos + 1) % EZ)]
        by_cell = jnp.stack([lower_x, upper_x, lower_y, upper_y, lower_z, upper_z])
        which_cell = jnp.argsort(where_cell, stable=True)
        return by_cell[:, which_cell].astype(jnp.int32)
    table = jax.vmap(one_device)(positions)
    return jnp.transpose(table, (1, 0, 2)).reshape(6, E_DEV * N_SPACE)


def draw_rims(key, part):
    base_key = key
    positions = cell_positions(base_key)
    slots = jnp.arange(EY * EZ, dtype=jnp.int32)
    ypos = slots // EZ
    zpos = slots % EZ
    lower = positions[:, cell_number(0, ypos, zpos)]
    upper = positions[:, cell_number(LX - 1, ypos, zpos)]
    table = jnp.stack([lower, upper], axis=1)
    return jnp.transpose(table, (1, 0, 2)).reshape(2, EY * EZ * N_SPACE).astype(jnp.int32)


def block_inverse(key, diag_low, diag_span):
    first_key, second_key = jax.random.split(key)
    shape = (NODES, NODES, E_DEV * N_SPACE)
    noise = jnp.clip(jax.random.normal(first_key, shape, jnp.float32), -3.0, 3.0)
    diagonal = diag_low + diag_span * jax.random.uniform(second_key, (NODES, E_DEV * N_SPACE), jnp.float32)
    skew = 0.02 * (noise - jnp.transpose(noise, (1, 0, 2)))
    return skew + jnp.eye(NODES, dtype=jnp.float32)[:, :, None] * diagonal[None]


def draw_inv_fine(key, part):
    key = jax.random.fold_in(key, 21)
    return block_inverse(key, 0.75, 0.2)


def draw_inv_coarse(key, part):
    key = jax.random.fold_in(key, 22)
    return block_inverse(key, 0.8, 0.17)


def level_of(stream_key, extent, pieces, least, top_value):
    def one(axis_at, shards_of):
        steps = jax.random.uniform(jax.random.fold_in(jax.random.fold_in(stream_key, 6), axis_at), (shards_of,), jnp.float32, least / len(pieces), top_value / len(pieces))
        return jnp.repeat(jnp.exp(steps), extent[axis_at] // shards_of).reshape((-1,) + (1,) * (len(extent) - axis_at - 1))

    level = one(*pieces[0])
    for cut in pieces[1:]:
        level = level * one(*cut)
    return level


def gaussian(rng, dims, deviation, limit, cuts=(), kind=jnp.bfloat16):
    gain = level_of(rng, dims, cuts, -0.22, 0.18) if cuts else 1.0
    entries = jax.random.normal(rng, dims, jnp.float32) * deviation * gain
    return jnp.minimum(jnp.maximum(entries, -limit), limit).astype(kind)


def setup_inputs(seed: int = 0) -> dict:
    arg_keys = jax.random.split(jax.random.key(seed), 11)
    states = gaussian(arg_keys[0], (SLICES, NODES, ELEMS), 1.0, 6.0, ((0, 32), (2, 8)), jnp.float32)
    initial = gaussian(arg_keys[1], (NODES, ELEMS), 1.0, 6.0, ((1, 8),), jnp.float32)
    source = gaussian(arg_keys[2], (STEPS, NODES, ELEMS), 0.5, 3.0, ((0, 32), (2, 8)), jnp.float32)
    mass = jnp.clip(0.85 + 0.14999998 * jax.random.uniform(arg_keys[3], (NODES, ELEMS), jnp.float32) ** level_of(arg_keys[3], (NODES, ELEMS), ((1, 8),), -0.2, 0.2), 0.85, 1.0)
    inv_fine = draw_inv_fine(jax.random.fold_in(arg_keys[10], 71), 0)
    inv_coarse = draw_inv_coarse(jax.random.fold_in(arg_keys[10], 71), 0)
    face_mats = gaussian(arg_keys[6], (6, FACE_NODES, FACE_NODES), FACE_NODES ** -0.5, 1.5, (), jnp.float32)
    face_coef = jnp.clip(jnp.exp(math.log(0.4) - 2.0794415 * jax.random.uniform(arg_keys[7], (6, ELEMS), jnp.float32) ** level_of(arg_keys[7], (6, ELEMS), ((1, 8),), -0.2, 0.2)), 0.05, 0.4)
    neighbours = draw_neighbours(jax.random.fold_in(arg_keys[10], 71), 0)
    rims = draw_rims(jax.random.fold_in(arg_keys[10], 71), 0)
    return {"states": states, "initial": initial, "source": source, "mass": mass, "inv_fine": inv_fine, "inv_coarse": inv_coarse, "face_mats": face_mats, "face_coef": face_coef, "neighbours": neighbours, "rims": rims}


step_fine = 0.1
step_coarse = 0.25


def reference(states, initial, source, mass, inv_fine, inv_coarse, face_mats, face_coef, neighbours, rims):
    node_count, elem_total = mass.shape
    per_device = elem_total // N_SPACE
    layer_size = rims.shape[1] // N_SPACE
    rim_blocks = rims.reshape(2, N_SPACE, layer_size)
    neighbour_blocks = neighbours.reshape(6, N_SPACE, per_device)

    def coupling(field):
        blocks = field.reshape(node_count, N_SPACE, per_device)
        low_rim = jnp.take_along_axis(blocks, rim_blocks[0][None], axis=2)
        high_rim = jnp.take_along_axis(blocks, rim_blocks[1][None], axis=2)
        extended = jnp.concatenate([blocks, jnp.roll(high_rim, 1, axis=1), jnp.roll(low_rim, -1, axis=1)], axis=2)
        summed = jnp.zeros((4, 4, 4, elem_total), field.dtype)
        for face_id in range(6):
            axis_id = face_id // 2
            own_side = 0 if face_id % 2 == 0 else 3
            far_side = 3 - own_side
            beside = jnp.take_along_axis(extended, neighbour_blocks[face_id][None], axis=2).reshape(4, 4, 4, elem_total)
            face_layer = lax.index_in_dim(beside, far_side, axis_id, keepdims=False).reshape(16, elem_total)
            flux_term = face_coef[face_id][None] * jnp.dot(face_mats[face_id], face_layer, precision=lax.Precision.HIGHEST)
            target = [slice(None), slice(None), slice(None), slice(None)]
            target[axis_id] = own_side
            summed = summed.at[tuple(target)].add(flux_term.reshape(4, 4, elem_total))
        return summed.reshape(node_count, elem_total)

    def advance(field, inverse, step_size):
        loaded = mass * field - step_size * coupling(field)
        return jnp.einsum("ije,je->ie", inverse, loaded, precision=lax.Precision.HIGHEST)

    fine_all = jax.vmap(lambda field: advance(field, inv_fine, step_fine))
    source_blocks = source.reshape(N_TM, STEP_SLICE, node_count, elem_total)

    def relax(start):
        kept = []
        current = start
        for step_id in range(STEP_SLICE - 1):
            current = fine_all(current) + source_blocks[:, step_id]
            kept.append(current)
        return jnp.stack(kept, axis=1), current

    first_pass, last_first = relax(states)
    moved = fine_all(last_first) + source_blocks[:, STEP_SLICE - 1]
    begin = jnp.concatenate([states[:1], moved[:-1]], axis=0)
    second_pass, last_second = relax(begin)
    arrived = fine_all(last_second) + source_blocks[:, STEP_SLICE - 1]
    defect = jnp.concatenate([(initial - states[0])[None], arrived[:-1] - begin[1:]], axis=0)

    def chain(carry, term):
        nested = advance(carry, inv_coarse, step_coarse) + term
        return nested, nested

    last_carry, carried = lax.scan(chain, jnp.zeros_like(states[0]), defect)
    c_points = begin + carried
    points, last_final = relax(c_points)
    return c_points, points.reshape(N_TM * (STEP_SLICE - 1), node_count, elem_total), defect
```

```python
import functools

import jax
import jax.numpy as jnp
import numpy as np
from jax import lax
from jax.experimental import pallas as pl
from jax.experimental.pallas import tpu as pltpu
from jax.sharding import PartitionSpec as P

step_fine = 0.1
step_coarse = 0.25
AXES = ("tm", "space")
VM = pl.BlockSpec(memory_space=pltpu.VMEM)
SM = pl.BlockSpec(memory_space=pltpu.SMEM)
HI = lax.Precision.HIGHEST


def device_index(x, y, z, core):
    x, y, z = x % 4, y % 4, z % 8
    return (y * 8 + (z // 2) * 2 + core) * 8 + x * 2 + z % 2


def pairs_of(rule):
    out = []
    for x in range(4):
        for y in range(4):
            for z in range(8):
                for core in range(2):
                    out.append((device_index(x, y, z, core), device_index(*rule(x, y, z, core))))
    return out


def space_up(x, y, z, core):
    return (x, y, z + 1, core) if z % 2 == 0 else (x + 1, y, z - 1, core)


def space_down(x, y, z, core):
    return (x, y, z - 1, core) if z % 2 == 1 else (x - 1, y, z + 1, core)


def next_slice(x, y, z, core):
    zh, zl = z // 2, z % 2
    t = (y * 8 + zh * 2 + core + 1) % 32
    return (x, t // 8, (t % 8) // 2 * 2 + zl, t % 2)


def then(first, second):
    return lambda x, y, z, core: second(*first(x, y, z, core))


def next_y(x, y, z, core):
    return (x, y + 1, z, core)


def halo_pair(x, y, z, core):
    way = 1 if (z % 2 == 0) == (core == 0) else -1
    return (x, y, z + way, core)


def halo_cross(x, y, z, core):
    way = 1 if (z % 2 == 0) == (core == 0) else -1
    return (x + (1 if z % 2 == 1 else -1), y, z + way, core)


def other_core(x, y, z, core):
    return (x, y, z, 1 - core)


UP, DOWN = pairs_of(space_up), pairs_of(space_down)
SLICE = pairs_of(next_slice)
SLICE_UP, SLICE_DOWN = pairs_of(then(next_slice, space_up)), pairs_of(then(next_slice, space_down))
YNEXT = pairs_of(next_y)
Y_UP, Y_DOWN = pairs_of(then(next_y, space_up)), pairs_of(then(next_y, space_down))
HALO_PAIR, HALO_CROSS = pairs_of(halo_pair), pairs_of(halo_cross)
CORE = pairs_of(other_core)
def group_pairs(far):
    def rule(x, y, z, core):
        return (x, y + 1 if core == 1 and z // 2 == 3 else y, z + 2 * far, core)

    return pairs_of(rule)


GROUP = [group_pairs(far) for far in range(4)]
FIRST_TO_LAST = [(device_index(x, 0, z, 0), device_index(x, 3, 6 + z, 1)) for x in range(4) for z in range(2)]


def send(array, pairs):
    return lax.ppermute(array, AXES, pairs)


def f32(*shape):
    return jax.ShapeDtypeStruct(shape, jnp.float32)


def vmem_f32(*shape):
    return pltpu.VMEM(shape, jnp.float32)


def pinned(array):
    return pltpu.with_memory_space_constraint(array, pltpu.VMEM)


def call(body, out_shapes, *args, specs=None, mib=8, scratch=()):
    return pl.pallas_call(
        body,
        out_shape=out_shapes,
        in_specs=specs or [VM] * len(args),
        out_specs=[VM] * len(out_shapes),
        scratch_shapes=list(scratch),
        compiler_params=pltpu.CompilerParams(vmem_limit_bytes=mib << 20),
    )(*args)


def first_half(shape):
    return lax.broadcasted_iota(jnp.int32, shape, len(shape) - 1) < 64


def roll_half(block):
    return pltpu.roll(block, 64, block.ndim - 1)


def merge(low, high):
    return jnp.where(first_half(low.shape), high, low)


def merge_far(low, high):
    return roll_half(jnp.where(first_half(low.shape), low, high))


def lane_take(block, index):
    return jnp.take_along_axis(block, index, axis=1, mode="promise_in_bounds")


def permute_lanes(block, hot):
    high = block.astype(jnp.bfloat16)
    rest = block - high.astype(jnp.float32)
    mid = rest.astype(jnp.bfloat16)
    low = (rest - mid.astype(jnp.float32)).astype(jnp.bfloat16)
    dot = functools.partial(jnp.dot, preferred_element_type=jnp.float32)
    return (dot(low, hot) + dot(mid, hot)) + dot(high, hot)


def hot_lanes(index_row):
    rows = lax.broadcasted_iota(jnp.int32, (256, 256), 0)
    return (rows == index_row).astype(jnp.float32).astype(jnp.bfloat16)


def flag_vector():
    tm = jnp.full((16,), lax.axis_index("tm"), jnp.int32)
    space = jnp.full((16,), lax.axis_index("space"), jnp.int32)
    at = jnp.arange(16, dtype=jnp.int32)
    core, z_high = tm & 1, (tm >> 1) & 3
    from_core = 1 - (at & 1)
    source = ((at >> 1) - from_core) & 3
    slot = ((z_high - source) & 3) + jnp.where(from_core != core, 4, 0)
    rest = [tm & 7, 1 - core, 1 - (space & 1), tm == 0, tm < 8, tm == 31]
    for i, value in enumerate(rest):
        slot = jnp.where(at == 8 + i, value.astype(jnp.int32), slot)
    return slot


def order_body(flag_ref, neighbours_ref, rims_ref, order_ref, beside_ref):
    table = neighbours_ref[...]
    parts = jnp.concatenate([table >> 4, table & 15], axis=0).astype(jnp.float32).astype(jnp.bfloat16)
    element = lax.broadcasted_iota(jnp.int32, (256, 64), 0)
    row_at = lax.broadcasted_iota(jnp.int32, (64, 64), 0)
    lane_at = lax.broadcasted_iota(jnp.int32, (64, 64), 1)
    orders, besides = [], []
    row = rims_ref[0:1]
    for layer in range(4):
        hot = (element == row).astype(jnp.float32).astype(jnp.bfloat16)
        found = jnp.dot(parts, hot, preferred_element_type=jnp.float32)
        found = (found[0:6] * 16 + found[6:12]).astype(jnp.int32)
        column = jnp.sum(jnp.where(row_at == lane_at, row, 0), axis=1, keepdims=True)
        local = [
            jnp.sum(jnp.where(column == found[f : f + 1], row_at, 0), axis=0, keepdims=True) + 64 * (layer & 1)
            for f in range(2, 6)
        ]
        orders.append(row)
        besides.append(jnp.concatenate(local, axis=0))
        row = rims_ref[1:2] if layer == 2 else found[1:2]
    order_ref[...] = jnp.concatenate(orders, axis=1)
    beside_ref[...] = jnp.concatenate(besides, axis=1).astype(jnp.float32)


def two_tiles(ref, block):
    ref[0] = block[:, 0:128]
    ref[1] = block[:, 128:256]


def prepare_body(
    flag_ref, index_ref, beside_ref, states_ref, initial_ref, source_ref, mass_ref, coef_ref,
    start_ref, initial_out_ref, src_ref, own_ref, up_ref, down_ref,
):
    hot = hot_lanes(index_ref[...])
    two_tiles(start_ref, permute_lanes(states_ref[0], hot))
    two_tiles(initial_out_ref, permute_lanes(initial_ref[...], hot))
    for k in range(4):
        src = permute_lanes(source_ref[k], hot)
        src_ref[k, 0] = src[:, 0:128]
        src_ref[k, 1] = src[:, 128:256]
        if k % 2 == 0:
            up_ref[80 + 8 * k : 96 + 8 * k] = src[48:64, 128:256]
            down_ref[80 + 8 * k : 96 + 8 * k] = src[0:16, 0:128]
    table = jnp.concatenate(
        [
            permute_lanes(mass_ref[...], hot),
            permute_lanes(jnp.concatenate([coef_ref[...], jnp.zeros((2, 256), jnp.float32)], axis=0), hot)[0:6],
            beside_ref[...],
            jnp.zeros((6, 256), jnp.float32),
        ],
        axis=0,
    )
    own_ref[...] = table
    up_ref[0:80] = table[:, 128:256]
    down_ref[0:80] = table[:, 0:128]


def restore_body(index_ref, corrected_ref, middle_ref, field_ref, final_ref, kept_ref, c_ref, f_ref, r_ref):
    hot = hot_lanes(index_ref[...])

    def back(ref):
        block = jnp.concatenate([ref[0], ref[1]], axis=1)
        high = block.astype(jnp.bfloat16)
        rest = block - high.astype(jnp.float32)
        mid = rest.astype(jnp.bfloat16)
        low = (rest - mid.astype(jnp.float32)).astype(jnp.bfloat16)

        def dot(part):
            return lax.dot_general(part, hot, (((1,), (1,)), ((), ())), preferred_element_type=jnp.float32)

        return (dot(low) + dot(mid)) + dot(high)

    c_ref[0] = back(corrected_ref)
    f_ref[0] = back(middle_ref)
    f_ref[1] = back(field_ref)
    f_ref[2] = back(final_ref)
    r_ref[0] = back(kept_ref)


def reorder_matrix_body(coarse, flag_ref, index_ref, block_ref, out_ref, pair_ref, cross_ref):
    hot = hot_lanes(index_ref[...])

    def turn(i, carry):
        at = pl.ds(pl.multiple_of(i * 8, 8), 8)
        out_ref[at] = permute_lanes(block_ref[at].reshape(512, 256), hot).reshape(8, 64, 256)
        return carry

    lax.fori_loop(0, 8, turn, 0)

    def lanes(tile, begin, rows):
        return out_ref[begin : begin + rows, :, 128 * tile : 128 * tile + 128]

    core_0, even = flag_ref[9] == 1, flag_ref[10] == 1
    first = first_half((4, 64, 128))
    packs = []
    if coarse:
        for i in range(0, 32, 4):
            packs.append(
                lambda i=i: (
                    jnp.where(first, roll_half(lanes(1, 32 + i, 4)), lanes(1, i, 4)),
                    jnp.where(first, lanes(0, i, 4), roll_half(lanes(0, 32 + i, 4))),
                )
            )
        for i in range(0, 8, 4):
            packs.append(
                lambda i=i: (
                    jnp.where(first, lanes(1, 56 + i, 4), roll_half(lanes(1, 48 + i, 4))),
                    jnp.where(first, roll_half(lanes(0, i, 4)), lanes(0, 8 + i, 4)),
                )
            )
    else:
        for i in range(0, 8, 4):
            packs.append(
                lambda i=i: (
                    jnp.where(first, roll_half(lanes(1, 56 + i, 4)), lanes(1, 48 + i, 4)),
                    jnp.where(first, lanes(0, i, 4), roll_half(lanes(0, 8 + i, 4))),
                )
            )
    half = len(packs) // 2
    for which in range(2):

        @pl.when(core_0 if which == 0 else jnp.logical_not(core_0))
        def _():
            for i in range(half):
                up, down = packs[which * half + i]()
                pair_ref[4 * i : 4 * i + 4] = jnp.where(even, up, down)
                cross_ref[4 * i : 4 * i + 4] = jnp.where(even, down, up)


def reorder_matrix(block, flags, index_row, coarse):
    half = 20 if coarse else 4
    return call(
        functools.partial(reorder_matrix_body, coarse),
        [vmem_f32(*block.shape), f32(half, 64, 128), f32(half, 64, 128)],
        flags, index_row, block, specs=[SM, VM, VM],
    )


def combine_rows(parts):
    sub = lax.broadcasted_iota(jnp.int32, (8, 128), 0)
    m4, m2, m1 = sub < 4, (sub & 3) < 2, (sub & 1) < 1
    stage = []
    for i in range(4):
        a, b = parts[i], parts[i + 4]
        stage.append(jnp.where(m4, a, b) + pltpu.roll(jnp.where(m4, b, a), 4, 0))

    def fold(a, b, mask, dist):
        other = jnp.where(mask, b, a)
        moved = jnp.where(mask, pltpu.roll(other, 8 - dist, 0), pltpu.roll(other, dist, 0))
        return jnp.where(mask, a, b) + moved

    r0 = fold(stage[0], stage[2], m2, 2)
    r1 = fold(stage[1], stage[3], m2, 2)
    return fold(r0, r1, m1, 1)


def fluxes(flux_mat, tiles):
    columns = []
    for tile in tiles:
        high = tile.astype(jnp.bfloat16)
        low = (tile - high.astype(jnp.float32)).astype(jnp.bfloat16)
        columns.append(jnp.concatenate([high, low, high, low], axis=0))
    stacked = jnp.concatenate(columns, axis=1)
    flux = jnp.dot(flux_mat, stacked, preferred_element_type=jnp.float32)
    return [flux[:, 128 * m : 128 * m + 128] for m in range(len(tiles))]


def loaded_tile(tile, flux, from_low, from_high, table, step):
    mass, index_1, coef_1, index_2, coef_2, coef = table
    coupling = coef_1 * lane_take(flux[32:96], index_1) + coef_2 * lane_take(flux[96:160], index_2)
    top = coupling[:16] + coef[0:1] * from_low
    bottom = coupling[48:] + coef[1:2] * from_high
    coupling = jnp.concatenate([top, coupling[16:48], bottom], axis=0)
    return mass * tile - step * coupling


def matvec_rows(block, load):
    parts = []
    for i in range(8):
        total = block[i, 0:8] * load[0:8]
        for j in range(1, 8):
            total = total + block[i, 8 * j : 8 * j + 8] * load[8 * j : 8 * j + 8]
        parts.append(total)
    return combine_rows(parts)


def march(count, step, edge, near, far, tables, mat, inv_ref, inv_full_ref, inv_near_ref, inv_far_ref, term, work_ref, done):
    first = first_half((16, 128))
    for turn in range(count):
        left = count - 1 - turn
        t1, t2 = work_ref[0], work_ref[1]
        if left == 2:
            flux = fluxes(mat, [t1, t2, near, far, edge])
        elif left == 1:
            flux = fluxes(mat, [t1, t2, near, far])
        else:
            flux = fluxes(mat, [t1, t2, near])
        lo, hi = [f[0:16] for f in flux], [f[16:32] for f in flux]
        loads = [
            loaded_tile(
                t1, flux[0], roll_half(jnp.where(first, lo[0], lo[2])),
                roll_half(jnp.where(first, hi[1], hi[0])), tables(0), step,
            ),
            loaded_tile(
                t2, flux[1], roll_half(jnp.where(first, lo[1], lo[0])),
                roll_half(jnp.where(first, hi[2], hi[1])), tables(1), step,
            ),
        ]
        if left >= 1:
            loads.append(
                loaded_tile(
                    near, flux[2], jnp.where(first, roll_half(lo[1]), lo[3]),
                    jnp.where(first, hi[3], roll_half(hi[0])), tables(2), step,
                )
            )
        if left == 2:
            loads.append(
                loaded_tile(
                    far, flux[3], jnp.where(first, lo[2], lo[4]), jnp.where(first, hi[4], hi[2]), tables(3), step
                )
            )

        def rows_turn(group, carry):
            rows = pl.ds(pl.multiple_of(group * 8, 8), 8)
            for m in range(2):
                value = matvec_rows(inv_ref[rows, :, 128 * m : 128 * m + 128], loads[m])
                work_ref[m, rows] = value + term(turn, m, rows)
            if left == 2:
                work_ref[2, rows] = matvec_rows(inv_full_ref[rows], loads[2]) + term(turn, 2, rows)
            return carry

        lax.fori_loop(0, 8, rows_turn, 0)
        if left == 2:
            face = [matvec_rows(inv_far_ref[8 * g : 8 * g + 8], loads[3]) + term(turn, 3, slice(8 * g, 8 * g + 8)) for g in range(2)]
            far = jnp.concatenate(face + [jnp.zeros((32, 128), jnp.float32)] + face, axis=0)
            near = work_ref[2]
        elif left == 1:
            face = [matvec_rows(inv_near_ref[8 * g : 8 * g + 8], loads[2]) + term(turn, 4, slice(8 * g, 8 * g + 8)) for g in range(2)]
            near = jnp.concatenate(face + [jnp.zeros((32, 128), jnp.float32)] + face, axis=0)
        done(turn)


def table_reader(refs):
    return lambda m: tuple(ref[m] for ref in refs)


def fine_body(
    count, near_at, switch, middle, flag_ref, v_ref, low_ref, high_ref, mass_ref, i1_ref, k1_ref, i2_ref, k2_ref, coef_ref, mat_ref,
    inv_ref, inv_near_ref, src_ref, table_low_ref, table_high_ref, *refs
):
    if switch:
        other_ref, other_low_ref, other_high_ref, out_ref = refs[:4]
        here = flag_ref[11] == 1
        out_ref[...] = jnp.where(here, other_ref[...], v_ref[...])
        low = jnp.where(here, other_low_ref[...], low_ref[...])
        high = jnp.where(here, other_high_ref[...], high_ref[...])
        if middle:
            refs[4][...] = out_ref[...]
    else:
        out_ref = refs[-1] if not middle else refs[-2]
        out_ref[...] = v_ref[...]
        low, high = low_ref[...], high_ref[...]
    near, far = merge(low, high), merge_far(low, high)
    first = first_half((8, 128))

    def term(turn, m, rows):
        if m == 4:
            at = near_at + rows.start
            return jnp.where(first, table_high_ref[at : at + 8], table_low_ref[at : at + 8])
        return src_ref[turn, m, rows]

    def done(turn):
        if middle and not switch and turn == 0:
            refs[-1][...] = out_ref[...]

    march(
        count, step_fine, None, near, far, table_reader((mass_ref, i1_ref, k1_ref, i2_ref, k2_ref, coef_ref)),
        mat_ref[...], inv_ref, None, inv_near_ref, None, term, out_ref, done,
    )


def window_body(
    count, first_slot, begins, first_group, pick,
    flag_ref, v_ref, low_ref, high_ref, mass_ref, i1_ref, k1_ref, i2_ref, k2_ref, coef_ref, mat_ref,
    inv_ref, inv_full_ref, inv_near_ref, inv_far_ref, term_ref, other_term_ref, kept_ref, begin_ref,
    out_ref, up_ref, down_ref, kept_out_ref, work_ref,
):
    low, high = low_ref[...], high_ref[...]
    work_ref[0], work_ref[1] = v_ref[0], v_ref[1]
    if begins:
        here = flag_ref[12] >= first_group
        low, high = jnp.where(here, 0.0, low), jnp.where(here, 0.0, high)
        work_ref[0:2] = jnp.where(here, 0.0, v_ref[...])
    near, far = merge(low[0:64], high[0:64]), merge_far(low[0:64], high[0:64])
    edge = jnp.concatenate([high[64:80], jnp.zeros((32, 128), jnp.float32), low[64:80]], axis=0)
    if pick:
        mine = flag_ref[8]
        if not begins:
            kept_out_ref[...] = kept_ref[...]
    first = first_half((8, 128))

    def term(turn, m, rows):
        slot = flag_ref[first_slot + turn]
        at = slot & 3

        def read(start):
            here = pl.ds(start, 8) if isinstance(start, int) else pl.ds(pl.multiple_of(start, 8), 8)
            return jnp.where(slot < 4, term_ref[at, here], other_term_ref[at, here])

        if m == 4:
            return jnp.where(first, read(128 + rows.start), read(176 + rows.start))
        return read((192 if m == 3 else 64 * m) + rows.start)

    def done(turn):
        if pick:

            @pl.when(mine == first_slot + turn)
            def _():
                slot = flag_ref[first_slot + turn]
                at = slot & 3
                for m in range(2):
                    rows = pl.ds(64 * m, 64)
                    kept_out_ref[m] = work_ref[m] + begin_ref[m]
                    kept_out_ref[2 + m] = jnp.where(slot < 4, term_ref[at, rows], other_term_ref[at, rows])

    march(
        count, step_coarse, edge, near, far, table_reader((mass_ref, i1_ref, k1_ref, i2_ref, k2_ref, coef_ref)),
        mat_ref[...], inv_ref, inv_full_ref, inv_near_ref, inv_far_ref, term, work_ref, done,
    )
    out_ref[0] = work_ref[0]
    out_ref[1] = work_ref[1]
    up_ref[0:64] = work_ref[1]
    up_ref[64:80] = work_ref[0, 48:64]
    down_ref[0:64] = work_ref[0]
    down_ref[64:80] = work_ref[1, 0:16]


def term_body(flag_ref, field_ref, handed_ref, initial_ref, states_ref, out_ref):
    last = flag_ref[13] == 1
    out_ref[...] = jnp.where(last, initial_ref[...] - states_ref[...], field_ref[...] - handed_ref[...])


def pack_terms_body(term_ref, low_ref, high_ref, out_ref):
    low, high = low_ref[...], high_ref[...]
    out_ref[0:64] = term_ref[0]
    out_ref[64:128] = term_ref[1]
    out_ref[128:192] = merge(low, high)
    out_ref[192:208] = roll_half(jnp.where(first_half((16, 128)), low[48:64], high[0:16]))


def stack_body(a_ref, b_ref, c_ref, d_ref, out_ref):
    for i, ref in enumerate((a_ref, b_ref, c_ref, d_ref)):
        out_ref[i] = ref[...]


def flux_constants():
    left, right = np.zeros((160, 96), np.float32), np.zeros((96, 64), np.float32)
    for face in range(6):
        axis, side = divmod(face, 2)
        for k in range(16):
            p, q = divmod(k, 4)
            node = [lambda d: 16 * d + 4 * p + q, lambda d: 16 * p + 4 * d + q, lambda d: 16 * p + 4 * q + d][axis]
            row = 16 * side + k if axis == 0 else 64 * axis - 32 + node(3 * side)
            left[row, 16 * face + k] = 1
            right[16 * face + k, node(3 - 3 * side)] = 1
    return left, right


def flux_body(mats_ref, left_ref, right_ref, out_ref):
    dot = functools.partial(jnp.dot, preferred_element_type=jnp.float32, precision=HI)
    parts = [dot(mats_ref[f], right_ref[16 * f : 16 * f + 16]) for f in range(6)]
    full = dot(left_ref[...], jnp.concatenate(parts, axis=0))
    high = full.astype(jnp.bfloat16)
    low = (full - high.astype(jnp.float32)).astype(jnp.bfloat16)
    out_ref[...] = jnp.concatenate([high, high, low, low], axis=1)


def tables_body(own_ref, low_ref, high_ref, mass_ref, i1_ref, k1_ref, i2_ref, k2_ref, coef_ref):
    node = lax.broadcasted_iota(jnp.int32, (64, 128), 0)
    along_b, along_c = (node >> 2) & 3, node & 3

    def spread(along, low, high):
        return jnp.where(along == 0, low, jnp.where(along == 3, high, jnp.zeros_like(low)))

    low, high = low_ref[0:80], high_ref[0:80]
    tiles = [own_ref[0:80, 0:128], own_ref[0:80, 128:256], merge(low, high), merge_far(low, high)]
    for m, tile in enumerate(tiles):
        index = tile[70:74].astype(jnp.int32)
        if m == 3:
            index = (index + 64) & 127
        mass_ref[m] = tile[0:64]
        coef_ref[m] = tile[64:72]
        i1_ref[m] = spread(along_b, index[0:1], index[1:2])
        i2_ref[m] = spread(along_c, index[2:3], index[3:4])
        k1_ref[m] = spread(along_b, tile[66:67], tile[67:68])
        k2_ref[m] = spread(along_c, tile[68:69], tile[69:70])


def stack_halo_body(pair_ref, cross_ref, out_ref):
    out_ref[0] = pair_ref[...]
    out_ref[1] = cross_ref[...]


def halo_body(coarse, flag_ref, pair_ref, cross_ref, other_ref, near_ref, full_ref=None, far_ref=None):
    half = 20 if coarse else 4
    core_0, even = flag_ref[9] == 1, flag_ref[10] == 1
    first = first_half((4, 64, 128))
    for part in range(2):
        for i in range(0, half, 4):
            rows = slice(i, i + 4)
            mine = core_0 if part == 0 else jnp.logical_not(core_0)
            pair = jnp.where(mine, pair_ref[rows], other_ref[0, rows])
            cross = jnp.where(mine, cross_ref[rows], other_ref[1, rows])
            low, high = jnp.where(even, cross, pair), jnp.where(even, pair, cross)
            at = half * part + i
            a, b = merge(low, high), merge_far(low, high)
            if not coarse:
                near_ref[at : at + 4], near_ref[8 + at : 12 + at] = a, b
            elif at < 32:
                full_ref[at : at + 4], full_ref[32 + at : 36 + at] = a, b
            else:
                far_ref[at - 32 : at - 28], far_ref[at - 24 : at - 20] = a, b
    if coarse:
        for i in range(0, 16, 4):
            near_ref[i : i + 4] = jnp.where(first, full_ref[i : i + 4], full_ref[48 + i : 52 + i])


def per_device(
    states, initial, source, mass, inv_fine, inv_coarse, face_mats, face_coef, neighbours, rims
):
    flags = flag_vector()
    order_row, beside = call(
        order_body, [jax.ShapeDtypeStruct((1, 256), jnp.int32), f32(4, 256)], flags, neighbours, rims, specs=[SM, VM, VM]
    )
    inv_f, fine_pair, fine_cross = reorder_matrix(inv_fine, flags, order_row, False)
    got_fine = send(fine_pair, HALO_PAIR), send(fine_cross, HALO_CROSS)
    pair = f32(2, 64, 128)
    start, first_value, src, table, up_table, down_table = call(
        prepare_body, [pair, pair, f32(4, 2, 64, 128), f32(80, 256), f32(112, 128), f32(112, 128)],
        flags, order_row, beside, states, initial, source, mass, face_coef, specs=[SM] + [VM] * 7,
    )
    low_table, high_table = send(up_table, UP), send(down_table, DOWN)
    start_low, start_high = send(start[1], UP), send(start[0], DOWN)
    inv_c, coarse_pair, coarse_cross = reorder_matrix(inv_coarse, flags, order_row, True)
    got_coarse = send(coarse_pair, HALO_PAIR), send(coarse_cross, HALO_CROSS)

    def join_halo(got, coarse, shapes):
        shape = (2,) + got[0].shape
        other = send(call(stack_halo_body, [f32(*shape)], *got)[0], CORE)
        return call(functools.partial(halo_body, coarse), shapes, flags, *got, other, specs=[SM] + [VM] * 3)

    (fine_near,) = join_halo(got_fine, False, [vmem_f32(16, 64, 128)])
    i32 = jax.ShapeDtypeStruct((4, 64, 128), jnp.int32)
    tables = call(
        tables_body, [f32(4, 64, 128), i32, f32(4, 64, 128), i32, f32(4, 64, 128), f32(4, 8, 128)],
        table, low_table, high_table,
    )
    left, right = flux_constants()
    mat = call(
        flux_body, [jax.ShapeDtypeStruct((160, 256), jnp.bfloat16)], face_mats, jnp.asarray(left), jnp.asarray(right)
    )[0]

    def fine_march(field, low, high, at, count, other=(), middle=False):
        operands = (
            flags, field, low, high, *tables, mat, pinned(inv_f), fine_near, src[at : at + count],
            low_table, high_table, *other,
        )
        return call(
            functools.partial(fine_body, count, 80 + 8 * at, bool(other), middle), [pair] * (2 if middle else 1),
            *operands, specs=[SM] + [VM] * (len(operands) - 1),
        )

    def exchange(field):
        return send(field[1], UP), send(field[0], DOWN)

    (field,) = fine_march(start, start_low, start_high, 0, 2)
    low, high = exchange(field)
    (handed,) = fine_march(field, low, high, 2, 2)
    arrived, low, high = send(handed, SLICE), send(handed[1], SLICE_UP), send(handed[0], SLICE_DOWN)

    field, begin = fine_march(arrived, low, high, 0, 2, (start, start_low, start_high), middle=True)
    low, high = exchange(field)
    (field,) = fine_march(field, low, high, 2, 2)
    far_start = send(start, FIRST_TO_LAST)
    next_term = call(term_body, [pair], flags, field, handed, first_value, far_start, specs=[SM] + [VM] * 4)[0]

    inv_near, inv_full, inv_far = join_halo(
        got_coarse, True, [vmem_f32(16, 64, 128), vmem_f32(64, 64, 128), vmem_f32(16, 64, 128)]
    )
    packed = call(pack_terms_body, [f32(208, 128)], next_term, *exchange(next_term))[0]
    terms = call(stack_body, [f32(4, 208, 128)], *(send(packed, pairs) for pairs in GROUP))[0]
    other_terms = send(terms, CORE)

    value, up, down = next_term, low_table[0:80], high_table[0:80]
    kept = None
    for turn in range(4):
        last = turn == 3
        for at, count in ((0, 3), (3, 3), (6, 2)):
            if at > 0:
                low, high = send(up, UP), send(down, DOWN)
            elif turn > 0:
                value, low, high = send(value, YNEXT), send(up, Y_UP), send(down, Y_DOWN)
            else:
                low, high = up, down
            value, up, down, kept = call(
                functools.partial(window_body, count, at, at == 0, 0 if turn == 0 else 1, last),
                [pair, f32(80, 128), f32(80, 128), f32(4, 64, 128)],
                flags, value, low, high, *tables, mat,
                pinned(inv_c), pinned(inv_full), pinned(inv_near), pinned(inv_far), terms, other_terms,
                kept if last and at > 0 else terms, begin,
                specs=[SM] + [VM] * 18, scratch=[pltpu.VMEM((3, 64, 128), jnp.float32)],
            )

    corrected = kept[0:2]
    low, high = exchange(corrected)
    field, middle = fine_march(corrected, low, high, 0, 2, middle=True)
    low, high = exchange(field)
    (final,) = fine_march(field, low, high, 2, 1)
    return call(
        restore_body, [f32(1, 64, 256), f32(3, 64, 256), f32(1, 64, 256)],
        order_row, corrected, middle, field, final, kept[2:4],
    )


def solution(mesh):
    return jax.shard_map(
        per_device,
        mesh=mesh,
        in_specs=(
            P("tm", None, "space"),
            P(None, "space"),
            P("tm", None, "space"),
            P(None, "space"),
            P(None, None, "space"),
            P(None, None, "space"),
            P(),
            P(None, "space"),
            P(None, "space"),
            P(None, "space"),
        ),
        out_specs=(P("tm", None, "space"), P("tm", None, "space"), P("tm", None, "space")),
        check_vma=False,
    )
```

```python
import functools

import jax
import jax.numpy as jnp
import numpy as np
from jax import lax
from jax.experimental import pallas as pl
from jax.experimental.pallas import tpu as pltpu
from jax.sharding import PartitionSpec as P

step_fine = 0.1
step_coarse = 0.25
AXES = ("tm", "space")
VM = pl.BlockSpec(memory_space=pltpu.VMEM)
SM = pl.BlockSpec(memory_space=pltpu.SMEM)
HI = lax.Precision.HIGHEST


def device_index(x, y, z, core):
    x, y, z = x % 4, y % 4, z % 8
    return (y * 8 + (z // 2) * 2 + core) * 8 + x * 2 + z % 2


def pairs_of(rule):
    out = []
    for x in range(4):
        for y in range(4):
            for z in range(8):
                for core in range(2):
                    out.append((device_index(x, y, z, core), device_index(*rule(x, y, z, core))))
    return out


def space_up(x, y, z, core):
    return (x, y, z + 1, core) if z % 2 == 0 else (x + 1, y, z - 1, core)


def space_down(x, y, z, core):
    return (x, y, z - 1, core) if z % 2 == 1 else (x - 1, y, z + 1, core)


def next_slice(x, y, z, core):
    zh, zl = z // 2, z % 2
    t = (y * 8 + zh * 2 + core + 1) % 32
    return (x, t // 8, (t % 8) // 2 * 2 + zl, t % 2)


def then(first, second):
    return lambda x, y, z, core: second(*first(x, y, z, core))


def next_y(x, y, z, core):
    return (x, y + 1, z, core)


def halo_pair(x, y, z, core):
    way = 1 if (z % 2 == 0) == (core == 0) else -1
    return (x, y, z + way, core)


def halo_cross(x, y, z, core):
    way = 1 if (z % 2 == 0) == (core == 0) else -1
    return (x + (1 if z % 2 == 1 else -1), y, z + way, core)


def other_core(x, y, z, core):
    return (x, y, z, 1 - core)


UP, DOWN = pairs_of(space_up), pairs_of(space_down)
SLICE = pairs_of(next_slice)
SLICE_UP, SLICE_DOWN = pairs_of(then(next_slice, space_up)), pairs_of(then(next_slice, space_down))
YNEXT = pairs_of(next_y)
Y_UP, Y_DOWN = pairs_of(then(next_y, space_up)), pairs_of(then(next_y, space_down))
HALO_PAIR, HALO_CROSS = pairs_of(halo_pair), pairs_of(halo_cross)
CORE = pairs_of(other_core)
def group_pairs(far):
    def rule(x, y, z, core):
        return (x, y + 1 if core == 1 and z // 2 == 3 else y, z + 2 * far, core)

    return pairs_of(rule)


GROUP = [group_pairs(far) for far in range(4)]
FIRST_TO_LAST = [(device_index(x, 0, z, 0), device_index(x, 3, 6 + z, 1)) for x in range(4) for z in range(2)]


def send(array, pairs):
    return lax.ppermute(array, AXES, pairs)


def f32(*shape):
    return jax.ShapeDtypeStruct(shape, jnp.float32)


def vmem_f32(*shape):
    return pltpu.VMEM(shape, jnp.float32)


def pinned(array):
    return pltpu.with_memory_space_constraint(array, pltpu.VMEM)


def call(body, out_shapes, *args, specs=None, mib=8, scratch=()):
    return pl.pallas_call(
        body,
        out_shape=out_shapes,
        in_specs=specs or [VM] * len(args),
        out_specs=[VM] * len(out_shapes),
        scratch_shapes=list(scratch),
        compiler_params=pltpu.CompilerParams(vmem_limit_bytes=mib << 20),
    )(*args)


def first_half(shape):
    return lax.broadcasted_iota(jnp.int32, shape, len(shape) - 1) < 64


def roll_half(block):
    return pltpu.roll(block, 64, block.ndim - 1)


def merge(low, high):
    return jnp.where(first_half(low.shape), high, low)


def merge_far(low, high):
    return roll_half(jnp.where(first_half(low.shape), low, high))


def lane_take(block, index):
    return jnp.take_along_axis(block, index, axis=1, mode="promise_in_bounds")


def permute_lanes(block, hot):
    high = block.astype(jnp.bfloat16)
    rest = block - high.astype(jnp.float32)
    mid = rest.astype(jnp.bfloat16)
    low = (rest - mid.astype(jnp.float32)).astype(jnp.bfloat16)
    dot = functools.partial(jnp.dot, preferred_element_type=jnp.float32)
    return (dot(low, hot) + dot(mid, hot)) + dot(high, hot)


def hot_lanes(index_row):
    rows = lax.broadcasted_iota(jnp.int32, (256, 256), 0)
    return (rows == index_row).astype(jnp.float32).astype(jnp.bfloat16)


def flag_vector():
    tm = jnp.full((16,), lax.axis_index("tm"), jnp.int32)
    space = jnp.full((16,), lax.axis_index("space"), jnp.int32)
    at = jnp.arange(16, dtype=jnp.int32)
    core, z_high = tm & 1, (tm >> 1) & 3
    from_core = 1 - (at & 1)
    source = ((at >> 1) - from_core) & 3
    slot = ((z_high - source) & 3) + jnp.where(from_core != core, 4, 0)
    rest = [tm & 7, 1 - core, 1 - (space & 1), tm == 0, tm < 8, tm == 31]
    for i, value in enumerate(rest):
        slot = jnp.where(at == 8 + i, value.astype(jnp.int32), slot)
    return slot


def layer_order(neighbours, rims):
    parts = jnp.concatenate([neighbours >> 4, neighbours & 15], axis=0).astype(jnp.float32).astype(jnp.bfloat16)
    element = lax.broadcasted_iota(jnp.int32, (256, 64), 0)
    row_at = lax.broadcasted_iota(jnp.int32, (64, 64), 0)
    lane_at = lax.broadcasted_iota(jnp.int32, (64, 64), 1)
    orders, besides = [], []
    row = rims[0:1]
    for layer in range(4):
        hot = (element == row).astype(jnp.float32).astype(jnp.bfloat16)
        found = jnp.dot(parts, hot, preferred_element_type=jnp.float32)
        found = (found[0:6] * 16 + found[6:12]).astype(jnp.int32)
        column = jnp.sum(jnp.where(row_at == lane_at, row, 0), axis=1, keepdims=True)
        local = [
            jnp.sum(jnp.where(column == found[f : f + 1], row_at, 0), axis=0, keepdims=True) + 64 * (layer & 1)
            for f in range(2, 6)
        ]
        orders.append(row)
        besides.append(jnp.concatenate(local, axis=0))
        row = rims[1:2] if layer == 2 else found[1:2]
    return jnp.concatenate(orders, axis=1), jnp.concatenate(besides, axis=1).astype(jnp.float32)


def two_tiles(ref, block):
    ref[0] = block[:, 0:128]
    ref[1] = block[:, 128:256]


def start_body(
    flag_ref, neighbours_hbm, rims_hbm, states_hbm, initial_hbm, source_hbm, mass_hbm, coef_hbm, inv_hbm,
    order_ref, spread_ref, start_ref, initial_out_ref, src_ref, own_ref, up_ref, down_ref, inv_ref, pair_ref, cross_ref,
    neighbours_ref, rims_ref, states_ref, initial_ref, source_ref, mass_ref, coef_ref, block_ref, sems,
):
    small = [
        (neighbours_hbm, neighbours_ref), (rims_hbm, rims_ref), (mass_hbm, mass_ref), (coef_hbm, coef_ref),
        (states_hbm, states_ref), (initial_hbm, initial_ref), (source_hbm, source_ref),
    ]
    copies = [pltpu.make_async_copy(a, b, sems.at[i]) for i, (a, b) in enumerate(small)]
    blocks = [
        pltpu.make_async_copy(inv_hbm.at[8 * i : 8 * i + 8], block_ref.at[8 * i : 8 * i + 8], sems.at[7 + i])
        for i in range(8)
    ]
    for copy in copies + blocks:
        copy.start()
    for i in range(16):
        spread_ref[i : i + 1] = jnp.full((1, 128), flag_ref[i], jnp.int32)
    copies[0].wait()
    copies[1].wait()
    order, beside = layer_order(neighbours_ref[...], rims_ref[...])
    order_ref[...] = order
    hot = hot_lanes(order)
    for i in range(8):
        blocks[i].wait()
        rows = permute_lanes(block_ref[8 * i : 8 * i + 8].reshape(512, 256), hot)
        inv_ref[8 * i : 8 * i + 8] = rows.reshape(8, 64, 256)
    for copy in copies[2:]:
        copy.wait()
    two_tiles(start_ref, permute_lanes(states_ref[0], hot))
    two_tiles(initial_out_ref, permute_lanes(initial_ref[...], hot))
    up_ref[0:64] = start_ref[1]
    down_ref[0:64] = start_ref[0]
    for k in range(4):
        src = permute_lanes(source_ref[k], hot)
        src_ref[k, 0] = src[:, 0:128]
        src_ref[k, 1] = src[:, 128:256]
        if k % 2 == 0:
            up_ref[64 + 8 * k : 80 + 8 * k] = src[48:64, 128:256]
            down_ref[64 + 8 * k : 80 + 8 * k] = src[0:16, 0:128]
    table = jnp.concatenate(
        [
            permute_lanes(mass_ref[...], hot),
            permute_lanes(jnp.concatenate([coef_ref[...], jnp.zeros((2, 256), jnp.float32)], axis=0), hot)[0:6],
            beside,
            jnp.zeros((6, 256), jnp.float32),
        ],
        axis=0,
    )
    own_ref[...] = table
    even = spread_ref[10:11] == 1

    def lanes(tile, begin):
        return inv_ref[begin : begin + 8, :, 128 * tile : 128 * tile + 128]

    first = first_half((8, 64, 128))
    up = jnp.where(first, roll_half(lanes(1, 56)), lanes(1, 48)).reshape(512, 128)
    down = jnp.where(first, lanes(0, 0), roll_half(lanes(0, 8))).reshape(512, 128)
    pair_ref[0:512] = jnp.where(even, up, down)
    cross_ref[0:512] = jnp.where(even, down, up)
    pair_ref[512:592] = jnp.where(even, table[:, 128:256], table[:, 0:128])
    cross_ref[512:592] = jnp.where(even, table[:, 0:128], table[:, 128:256])


def restore_body(index_ref, corrected_ref, middle_ref, field_ref, final_ref, kept_ref, c_ref, f_ref, r_ref):
    hot = hot_lanes(index_ref[...])

    def back(ref):
        block = jnp.concatenate([ref[0], ref[1]], axis=1)
        high = block.astype(jnp.bfloat16)
        rest = block - high.astype(jnp.float32)
        mid = rest.astype(jnp.bfloat16)
        low = (rest - mid.astype(jnp.float32)).astype(jnp.bfloat16)

        def dot(part):
            return lax.dot_general(part, hot, (((1,), (1,)), ((), ())), preferred_element_type=jnp.float32)

        return (dot(low) + dot(mid)) + dot(high)

    c_ref[0] = back(corrected_ref)
    f_ref[0] = back(middle_ref)
    f_ref[1] = back(field_ref)
    f_ref[2] = back(final_ref)
    r_ref[0] = back(kept_ref)


def reorder_matrix_body(flag_ref, index_ref, block_ref, out_ref, pair_ref, cross_ref):
    hot = hot_lanes(index_ref[...])

    def turn(i, carry):
        at = pl.ds(pl.multiple_of(i * 8, 8), 8)
        out_ref[at] = permute_lanes(block_ref[at].reshape(512, 256), hot).reshape(8, 64, 256)
        return carry

    lax.fori_loop(0, 8, turn, 0)

    def lanes(tile, begin):
        return out_ref[begin : begin + 4, :, 128 * tile : 128 * tile + 128]

    core_0, even = flag_ref[9:10] == 1, flag_ref[10:11] == 1
    first = first_half((4, 64, 128))

    def pack(at):
        if at < 32:
            return (
                jnp.where(first, roll_half(lanes(1, 32 + at)), lanes(1, at)),
                jnp.where(first, lanes(0, at), roll_half(lanes(0, 32 + at))),
            )
        at -= 32
        return (
            jnp.where(first, lanes(1, 56 + at), roll_half(lanes(1, 48 + at))),
            jnp.where(first, roll_half(lanes(0, at)), lanes(0, 8 + at)),
        )

    for i in range(0, 20, 4):
        (up, down), (far_up, far_down) = pack(i), pack(20 + i)
        up, down = jnp.where(core_0, up, far_up), jnp.where(core_0, down, far_down)
        pair_ref[i : i + 4] = jnp.where(even, up, down)
        cross_ref[i : i + 4] = jnp.where(even, down, up)


def combine_rows(parts):
    sub = lax.broadcasted_iota(jnp.int32, (8, 128), 0)
    m4, m2, m1 = sub < 4, (sub & 3) < 2, (sub & 1) < 1
    stage = []
    for i in range(4):
        a, b = parts[i], parts[i + 4]
        stage.append(jnp.where(m4, a, b) + pltpu.roll(jnp.where(m4, b, a), 4, 0))

    def fold(a, b, mask, dist):
        other = jnp.where(mask, b, a)
        moved = jnp.where(mask, pltpu.roll(other, 8 - dist, 0), pltpu.roll(other, dist, 0))
        return jnp.where(mask, a, b) + moved

    r0 = fold(stage[0], stage[2], m2, 2)
    r1 = fold(stage[1], stage[3], m2, 2)
    return fold(r0, r1, m1, 1)


def face_rows(tile):
    sub = lax.broadcasted_iota(jnp.int32, (8, 128), 0)
    rows = []
    for a in range(4):
        even, odd = tile[16 * a : 16 * a + 8], tile[16 * a + 8 : 16 * a + 16]
        rows.append(pltpu.roll(jnp.where(sub < 4, even, odd), 4, 0))
    ends = ((sub + 1) & 3) < 2
    for a in range(4):
        even, odd = tile[16 * a : 16 * a + 8], tile[16 * a + 8 : 16 * a + 16]
        rows.append(jnp.where(ends, even, pltpu.roll(odd, 2, 0)))
    return jnp.concatenate(rows, axis=0)


def loaded_tiles(flux_mat, items, step):
    columns = []
    for tile, from_low, from_high, (mass, index, coef, ends) in items:
        moved = coef * lane_take(face_rows(tile), index)
        rows = jnp.concatenate([moved, ends[0:1] * from_low, ends[1:2] * from_high], axis=0)
        high = rows.astype(jnp.bfloat16)
        low = (rows - high.astype(jnp.float32)).astype(jnp.bfloat16)
        columns.append(jnp.concatenate([high, low], axis=0))
    both = jnp.dot(flux_mat, jnp.concatenate(columns, axis=1), preferred_element_type=jnp.float32)
    coupling = both[0:64] + both[64:128]
    return [
        item[3][0] * item[0] - step * coupling[:, 128 * m : 128 * m + 128] for m, item in enumerate(items)
    ]


def matvec_rows(block, load):
    parts = []
    for i in range(8):
        total = block[i, 0:8] * load[0:8]
        for j in range(1, 8):
            total = total + block[i, 8 * j : 8 * j + 8] * load[8 * j : 8 * j + 8]
        parts.append(total)
    return combine_rows(parts)


def march(count, step, edge, near, far, tables, mat, inv_ref, inv_full_ref, inv_near_ref, inv_far_ref, term, work_ref, done):
    first = first_half((16, 128))
    for turn in range(count):
        left = count - 1 - turn
        t1, t2 = work_ref[0], work_ref[1]
        tiles = [t1, t2, near] + ([far] if left >= 1 else []) + ([edge] if left == 2 else [])
        hi, lo = [t[0:16] for t in tiles], [t[48:64] for t in tiles]
        items = [
            (t1, roll_half(jnp.where(first, lo[0], lo[2])), roll_half(jnp.where(first, hi[1], hi[0])), tables(0)),
            (t2, roll_half(jnp.where(first, lo[1], lo[0])), roll_half(jnp.where(first, hi[2], hi[1])), tables(1)),
        ]
        if left >= 1:
            items.append(
                (near, jnp.where(first, roll_half(lo[1]), lo[3]), jnp.where(first, hi[3], roll_half(hi[0])), tables(2))
            )
        if left == 2:
            items.append((far, jnp.where(first, lo[2], lo[4]), jnp.where(first, hi[4], hi[2]), tables(3)))
        loads = loaded_tiles(mat, items, step)

        def rows_turn(group, carry):
            rows = pl.ds(pl.multiple_of(group * 8, 8), 8)
            for m in range(2):
                value = matvec_rows(inv_ref[rows, :, 128 * m : 128 * m + 128], loads[m])
                work_ref[m, rows] = value + term(turn, m, rows)
            if left == 2:
                work_ref[2, rows] = matvec_rows(inv_full_ref[rows], loads[2]) + term(turn, 2, rows)
            return carry

        lax.fori_loop(0, 8, rows_turn, 0)
        if left == 2:
            face = [matvec_rows(inv_far_ref[8 * g : 8 * g + 8], loads[3]) + term(turn, 3, slice(8 * g, 8 * g + 8)) for g in range(2)]
            far = jnp.concatenate(face + [jnp.zeros((32, 128), jnp.float32)] + face, axis=0)
            near = work_ref[2]
        elif left == 1:
            face = [matvec_rows(inv_near_ref[8 * g : 8 * g + 8], loads[2]) + term(turn, 4, slice(8 * g, 8 * g + 8)) for g in range(2)]
            near = jnp.concatenate(face + [jnp.zeros((32, 128), jnp.float32)] + face, axis=0)
        done(turn)


def table_reader(refs):
    return lambda m: tuple(ref[m] for ref in refs)


def fine_body(
    count, near_at, switch, middle, flag_ref, v_ref, low_ref, high_ref, mass_ref, index_ref, face_ref, coef_ref, mat_ref,
    inv_ref, inv_near_ref, src_ref, start_low_ref, start_high_ref, *refs
):
    if switch:
        other_ref, out_ref = refs[:2]
        here = flag_ref[11:12] == 1
        out_ref[...] = jnp.where(here, other_ref[...], v_ref[...])
        low = jnp.where(here, start_low_ref[0:64], low_ref[...])
        high = jnp.where(here, start_high_ref[0:64], high_ref[...])
        if middle:
            refs[2][...] = out_ref[...]
    else:
        out_ref = refs[-1] if not middle else refs[-2]
        out_ref[...] = v_ref[...]
        low, high = low_ref[0:64], high_ref[0:64]
    near, far = merge(low, high), merge_far(low, high)
    first = first_half((8, 128))

    def term(turn, m, rows):
        if m == 4:
            at = near_at + rows.start
            return jnp.where(first, start_high_ref[at : at + 8], start_low_ref[at : at + 8])
        return src_ref[turn, m, rows]

    def done(turn):
        if middle and not switch and turn == 0:
            refs[-1][...] = out_ref[...]

    march(
        count, step_fine, None, near, far, table_reader((mass_ref, index_ref, face_ref, coef_ref)),
        mat_ref[...], inv_ref, None, inv_near_ref, None, term, out_ref, done,
    )


def window_body(
    count, first_slot, begins, first_group, pick,
    flag_ref, v_ref, low_ref, high_ref, mass_ref, index_ref, face_ref, coef_ref, mat_ref,
    inv_ref, inv_full_ref, inv_near_ref, inv_far_ref, term_ref, *refs
):
    if pick:
        begin_ref = refs[0]
        kept_out_ref = refs[-2]
    out_ref, up_ref, down_ref = refs[-5:-2] if pick else refs[-4:-1]
    work_ref = refs[-1]
    low, high = low_ref[...], high_ref[...]
    work_ref[0], work_ref[1] = v_ref[0], v_ref[1]
    if begins:
        here = flag_ref[12:13] >= first_group
        low, high = jnp.where(here, 0.0, low), jnp.where(here, 0.0, high)
        work_ref[0:2] = jnp.where(here, 0.0, v_ref[...])
    near, far = merge(low[0:64], high[0:64]), merge_far(low[0:64], high[0:64])
    edge = jnp.concatenate([high[64:80], jnp.zeros((32, 128), jnp.float32), low[64:80]], axis=0)
    if pick:
        kept_out_ref[...] = refs[1][...] if first_slot > 0 else jnp.zeros((4, 64, 128), jnp.float32)
    first = first_half((8, 128))

    def term(turn, m, rows):
        at = first_slot + turn
        if m == 4:
            here, there = 128 + rows.start, 176 + rows.start
            return jnp.where(first, term_ref[at, here : here + 8], term_ref[at, there : there + 8])
        if m == 3:
            return term_ref[at, 192 + rows.start : 200 + rows.start]
        return term_ref[at, pl.ds(pl.multiple_of(64 * m + rows.start, 8), 8)]

    def done(turn):
        if pick:
            mine = flag_ref[8:9] == first_slot + turn
            for m in range(2):
                rows = slice(64 * m, 64 * m + 64)
                kept_out_ref[m] = jnp.where(mine, work_ref[m] + begin_ref[m], kept_out_ref[m])
                kept_out_ref[2 + m] = jnp.where(mine, term_ref[first_slot + turn, rows], kept_out_ref[2 + m])

    march(
        count, step_coarse, edge, near, far, table_reader((mass_ref, index_ref, face_ref, coef_ref)),
        mat_ref[...], inv_ref, inv_full_ref, inv_near_ref, inv_far_ref, term, work_ref, done,
    )
    out_ref[0] = work_ref[0]
    out_ref[1] = work_ref[1]
    up_ref[0:64] = work_ref[1]
    up_ref[64:80] = work_ref[0, 48:64]
    down_ref[0:64] = work_ref[0]
    down_ref[64:80] = work_ref[1, 0:16]


def term_body(flag_ref, field_ref, handed_ref, initial_ref, states_ref, out_ref):
    last = flag_ref[13:14] == 1
    out_ref[...] = jnp.where(last, initial_ref[...] - states_ref[...], field_ref[...] - handed_ref[...])


def pack_terms_body(term_ref, low_ref, high_ref, out_ref):
    low, high = low_ref[...], high_ref[...]
    out_ref[0:64] = term_ref[0]
    out_ref[64:128] = term_ref[1]
    out_ref[128:192] = merge(low, high)
    out_ref[192:208] = roll_half(jnp.where(first_half((16, 128)), low[48:64], high[0:16]))


def stack_body(a_ref, b_ref, c_ref, d_ref, out_ref):
    for i, ref in enumerate((a_ref, b_ref, c_ref, d_ref)):
        out_ref[i] = ref[...]


def flux_constants():
    left, right = np.zeros((64, 96), np.float32), np.zeros((96, 96), np.float32)
    for face in range(6):
        axis, side = divmod(face, 2)
        for k in range(16):
            p, q = divmod(k, 4)
            node = [lambda d: 16 * d + 4 * p + q, lambda d: 16 * p + 4 * d + q, lambda d: 16 * p + 4 * q + d][axis]
            left[node(3 * side), 16 * face + k] = 1
    for row in range(96):
        group, sub = divmod(row, 8)
        if row >= 64:
            face, k = divmod(row - 64, 16)
        elif row < 32:
            face, k = 2 + sub // 4, 4 * group + sub % 4
        else:
            node = 16 * (group - 4) + (sub if sub % 4 in (0, 3) else 8 + (sub - 2) % 8)
            face, k = (4 if node % 4 == 3 else 5), node // 4
        right[16 * face + k, row] = 1
    return left, right


def flux_body(mats_ref, left_ref, right_ref, out_ref):
    dot = functools.partial(jnp.dot, preferred_element_type=jnp.float32, precision=HI)
    parts = [dot(mats_ref[f], right_ref[16 * f : 16 * f + 16]) for f in range(6)]
    full = dot(left_ref[...], jnp.concatenate(parts, axis=0))
    high = full.astype(jnp.bfloat16)
    low = (full - high.astype(jnp.float32)).astype(jnp.bfloat16)
    out_ref[...] = jnp.concatenate(
        [jnp.concatenate([high, high], axis=1), jnp.concatenate([low, low], axis=1)], axis=0
    )


def tables_body(flag_ref, own_ref, pair_ref, cross_ref, inv_near_ref, mass_ref, index_ref, face_ref, coef_ref):
    row = lax.broadcasted_iota(jnp.int32, (64, 128), 0)
    along_b = row < 32
    second = jnp.where(along_b, (row >> 2) & 1, 1 - (row & 1)) == 1
    even = flag_ref[10:11] == 1

    def beside(begin, end):
        pair, cross = pair_ref[begin:end], cross_ref[begin:end]
        return jnp.where(even, cross, pair), jnp.where(even, pair, cross)

    for i in range(8):
        low, high = beside(64 * i, 64 * i + 64)
        inv_near_ref[i], inv_near_ref[8 + i] = merge(low, high), merge_far(low, high)
    low, high = beside(512, 592)
    tiles = [own_ref[0:80, 0:128], own_ref[0:80, 128:256], merge(low, high), merge_far(low, high)]
    for m, tile in enumerate(tiles):
        index = tile[70:74].astype(jnp.int32)
        if m == 3:
            index = (index + 64) & 127

        def spread(rows):
            return jnp.where(along_b, jnp.where(second, rows[1:2], rows[0:1]), jnp.where(second, rows[3:4], rows[2:3]))

        mass_ref[m] = tile[0:64]
        coef_ref[m] = tile[64:72]
        index_ref[m] = spread(index)
        face_ref[m] = spread(tile[66:70])


def sort_terms_body(flag_ref, own_ref, other_ref, out_ref):
    for j in range(8):
        slot = flag_ref[j]

        @pl.when(slot < 4)
        def _():
            out_ref[j] = own_ref[slot & 3]

        @pl.when(slot >= 4)
        def _():
            out_ref[j] = other_ref[slot & 3]


def join_halo_body(*refs):
    out_ref = refs[-1]
    for i in range(4):
        out_ref[0, 5 * i : 5 * i + 5] = refs[2 * i][...]
        out_ref[1, 5 * i : 5 * i + 5] = refs[2 * i + 1][...]


def halo_body(flag_ref, own_ref, other_ref, near_ref, full_ref, far_ref):
    core_0, even = flag_ref[9:10] == 1, flag_ref[10:11] == 1
    first = first_half((4, 64, 128))
    for part in range(2):
        for i in range(0, 20, 4):
            rows = slice(i, i + 4)
            mine, others = (own_ref[0, rows], own_ref[1, rows]), (other_ref[0, rows], other_ref[1, rows])
            yes, no = (mine, others) if part == 0 else (others, mine)
            pair, cross = jnp.where(core_0, yes[0], no[0]), jnp.where(core_0, yes[1], no[1])
            low, high = jnp.where(even, cross, pair), jnp.where(even, pair, cross)
            at = 20 * part + i
            a, b = merge(low, high), merge_far(low, high)
            if at < 32:
                full_ref[at : at + 4], full_ref[32 + at : 36 + at] = a, b
            else:
                far_ref[at - 32 : at - 28], far_ref[at - 24 : at - 20] = a, b
    for i in range(0, 16, 4):
        near_ref[i : i + 4] = jnp.where(first, full_ref[i : i + 4], full_ref[48 + i : 52 + i])


def per_device(
    states, initial, source, mass, inv_fine, inv_coarse, face_mats, face_coef, neighbours, rims
):
    flags = flag_vector()
    pair = f32(2, 64, 128)
    hbm = pl.BlockSpec(memory_space=pltpu.HBM)
    inputs = (neighbours, rims, states, initial, source, mass, face_coef, inv_fine)
    scratch = [
        pltpu.VMEM(a.shape, a.dtype)
        for a in (neighbours, rims, states, initial, source, mass, face_coef, inv_fine)
    ]
    order_row, spread, start, first_value, src, table, up_start, down_start, inv_f, fine_pair, fine_cross = call(
        start_body,
        [
            jax.ShapeDtypeStruct((1, 256), jnp.int32), jax.ShapeDtypeStruct((16, 128), jnp.int32), pair, pair,
            f32(4, 2, 64, 128), f32(80, 256), f32(96, 128), f32(96, 128), vmem_f32(64, 64, 256),
            f32(592, 128), f32(592, 128),
        ],
        flags, *(pltpu.with_memory_space_constraint(a, pltpu.HBM) for a in inputs), specs=[SM] + [hbm] * 8, scratch=scratch + [pltpu.SemaphoreType.DMA((15,))], mib=20,
    )
    low_start, high_start = send(up_start, UP), send(down_start, DOWN)
    got_pair, got_cross = send(fine_pair, HALO_PAIR), send(fine_cross, HALO_CROSS)
    inv_c, coarse_pair, coarse_cross = call(
        reorder_matrix_body, [vmem_f32(64, 64, 256), f32(20, 64, 128), f32(20, 64, 128)], spread, order_row, inv_coarse
    )
    got_coarse = []

    def with_part(part, *arrived):
        rows = slice(5 * part, 5 * part + 5)
        pair, cross, *arrived = lax.optimization_barrier((coarse_pair[rows], coarse_cross[rows], *arrived))
        got_coarse.append((send(pair, HALO_PAIR), send(cross, HALO_CROSS)))
        return arrived

    far_start = send(start, FIRST_TO_LAST)
    low_start, high_start, got_pair, got_cross, far_start = with_part(
        0, low_start, high_start, got_pair, got_cross, far_start
    )
    fine_near, *tables = call(
        tables_body,
        [
            vmem_f32(16, 64, 128), f32(4, 64, 128), jax.ShapeDtypeStruct((4, 64, 128), jnp.int32), f32(4, 64, 128),
            f32(4, 8, 128),
        ],
        spread, table, got_pair, got_cross,
    )
    left, right = flux_constants()
    mat = call(
        flux_body, [jax.ShapeDtypeStruct((128, 192), jnp.bfloat16)], face_mats, jnp.asarray(left), jnp.asarray(right)
    )[0]

    def fine_march(field, low, high, at, count, other=(), middle=False):
        operands = (
            spread, field, low, high, *tables, mat, pinned(inv_f), fine_near, src[at : at + count],
            low_start, high_start, *other,
        )
        return call(
            functools.partial(fine_body, count, 64 + 8 * at, bool(other), middle), [pair] * (2 if middle else 1),
            *operands,
        )

    def exchange(field):
        return send(field[1], UP), send(field[0], DOWN)

    (field,) = fine_march(start, low_start, high_start, 0, 2)
    low, high = with_part(1, *exchange(field))
    (handed,) = fine_march(field, low, high, 2, 2)
    arrived, low, high = with_part(2, send(handed, SLICE), send(handed[1], SLICE_UP), send(handed[0], SLICE_DOWN))

    field, begin = fine_march(arrived, low, high, 0, 2, (start,), middle=True)
    low, high = with_part(3, *exchange(field))
    (field,) = fine_march(field, low, high, 2, 2)
    next_term = call(term_body, [pair], spread, field, handed, first_value, far_start)[0]

    joined = call(join_halo_body, [f32(2, 20, 64, 128)], *(part for parts in got_coarse for part in parts))[0]
    inv_near, inv_full, inv_far = call(
        halo_body, [vmem_f32(16, 64, 128), vmem_f32(64, 64, 128), vmem_f32(16, 64, 128)],
        spread, joined, send(joined, CORE),
    )
    packed = call(pack_terms_body, [f32(208, 128)], next_term, *exchange(next_term))[0]
    terms = call(stack_body, [f32(4, 208, 128)], *(send(packed, pairs) for pairs in GROUP))[0]
    terms = call(sort_terms_body, [f32(8, 208, 128)], flags, terms, send(terms, CORE), specs=[SM, VM, VM])[0]

    value, up, down = next_term, low_start, high_start
    picked = []
    for turn in range(4):
        last = turn == 3
        for at, count in ((0, 3), (3, 3), (6, 2)):
            if at > 0:
                low, high = send(up, UP), send(down, DOWN)
            elif turn > 0:
                value, low, high = send(value, YNEXT), send(up, Y_UP), send(down, Y_DOWN)
            else:
                low, high = up, down
            value, up, down, *picked = call(
                functools.partial(window_body, count, at, at == 0, 0 if turn == 0 else 1, last),
                [pair, f32(80, 128), f32(80, 128)] + [f32(4, 64, 128)] * last,
                spread, value, low, high, *tables, mat,
                pinned(inv_c), pinned(inv_full), pinned(inv_near), pinned(inv_far), pinned(terms),
                *([begin] * last), *picked, scratch=[pltpu.VMEM((3, 64, 128), jnp.float32)],
            )
    kept = picked[0]

    corrected = kept[0:2]
    low, high = exchange(corrected)
    field, middle = fine_march(corrected, low, high, 0, 2, middle=True)
    low, high = exchange(field)
    (final,) = fine_march(field, low, high, 2, 1)
    return call(
        restore_body, [f32(1, 64, 256), f32(3, 64, 256), f32(1, 64, 256)],
        order_row, corrected, middle, field, final, kept[2:4],
    )


def solution(mesh):
    return jax.shard_map(
        per_device,
        mesh=mesh,
        in_specs=(
            P("tm", None, "space"),
            P(None, "space"),
            P("tm", None, "space"),
            P(None, "space"),
            P(None, None, "space"),
            P(None, None, "space"),
            P(),
            P(None, "space"),
            P(None, "space"),
            P(None, "space"),
        ),
        out_specs=(P("tm", None, "space"), P("tm", None, "space"), P("tm", None, "space")),
        check_vma=False,
    )
```

```python
import functools

import jax
import jax.numpy as jnp
import numpy as np
from jax import lax
from jax.experimental import pallas as pl
from jax.experimental.pallas import tpu as pltpu
from jax.sharding import PartitionSpec as P

step_fine = 0.1
step_coarse = 0.25
AXES = ("tm", "space")
VM = pl.BlockSpec(memory_space=pltpu.VMEM)
SM = pl.BlockSpec(memory_space=pltpu.SMEM)
HI = lax.Precision.HIGHEST


def device_index(x, y, z, core):
    x, y, z = x % 4, y % 4, z % 8
    return (y * 8 + (z // 2) * 2 + core) * 8 + x * 2 + z % 2


def pairs_of(rule):
    out = []
    for x in range(4):
        for y in range(4):
            for z in range(8):
                for core in range(2):
                    out.append((device_index(x, y, z, core), device_index(*rule(x, y, z, core))))
    return out


def space_up(x, y, z, core):
    return (x, y, z + 1, core) if z % 2 == 0 else (x + 1, y, z - 1, core)


def space_down(x, y, z, core):
    return (x, y, z - 1, core) if z % 2 == 1 else (x - 1, y, z + 1, core)


def next_slice(x, y, z, core):
    zh, zl = z // 2, z % 2
    t = (y * 8 + zh * 2 + core + 1) % 32
    return (x, t // 8, (t % 8) // 2 * 2 + zl, t % 2)


def then(first, second):
    return lambda x, y, z, core: second(*first(x, y, z, core))


def next_y(x, y, z, core):
    return (x, y + 1, z, core)


def halo_pair(x, y, z, core):
    way = 1 if (z % 2 == 0) == (core == 0) else -1
    return (x, y, z + way, core)


def halo_cross(x, y, z, core):
    way = 1 if (z % 2 == 0) == (core == 0) else -1
    return (x + (1 if z % 2 == 1 else -1), y, z + way, core)


def other_core(x, y, z, core):
    return (x, y, z, 1 - core)


UP, DOWN = pairs_of(space_up), pairs_of(space_down)
SLICE = pairs_of(next_slice)
SLICE_UP, SLICE_DOWN = pairs_of(then(next_slice, space_up)), pairs_of(then(next_slice, space_down))
YNEXT = pairs_of(next_y)
Y_UP, Y_DOWN = pairs_of(then(next_y, space_up)), pairs_of(then(next_y, space_down))
HALO_PAIR, HALO_CROSS = pairs_of(halo_pair), pairs_of(halo_cross)
CORE = pairs_of(other_core)
def group_pairs(far):
    def rule(x, y, z, core):
        return (x, y + 1 if core == 1 and z // 2 == 3 else y, z + 2 * far, core)

    return pairs_of(rule)


GROUP = [group_pairs(far) for far in range(4)]
FIRST_TO_LAST = [(device_index(x, 0, z, 0), device_index(x, 3, 6 + z, 1)) for x in range(4) for z in range(2)]


def send(array, pairs):
    return lax.ppermute(array, AXES, pairs)


def f32(*shape):
    return jax.ShapeDtypeStruct(shape, jnp.float32)


def vmem_f32(*shape):
    return pltpu.VMEM(shape, jnp.float32)


def pinned(array):
    return pltpu.with_memory_space_constraint(array, pltpu.VMEM)


def call(body, out_shapes, *args, specs=None, mib=8, scratch=(), cost=None):
    return pl.pallas_call(
        body,
        out_shape=out_shapes,
        in_specs=specs or [VM] * len(args),
        out_specs=[VM] * len(out_shapes),
        scratch_shapes=list(scratch),
        compiler_params=pltpu.CompilerParams(vmem_limit_bytes=mib << 20),
        cost_estimate=cost,
    )(*args)


def first_half(shape):
    return lax.broadcasted_iota(jnp.int32, shape, len(shape) - 1) < 64


def roll_half(block):
    return pltpu.roll(block, 64, block.ndim - 1)


def merge(low, high):
    return jnp.where(first_half(low.shape), high, low)


def merge_far(low, high):
    return roll_half(jnp.where(first_half(low.shape), low, high))


def lane_take(block, index):
    return jnp.take_along_axis(block, index, axis=1, mode="promise_in_bounds")


def permute_lanes(block, hot):
    high = block.astype(jnp.bfloat16)
    rest = block - high.astype(jnp.float32)
    mid = rest.astype(jnp.bfloat16)
    low = (rest - mid.astype(jnp.float32)).astype(jnp.bfloat16)
    dot = functools.partial(jnp.dot, preferred_element_type=jnp.float32)
    return (dot(low, hot) + dot(mid, hot)) + dot(high, hot)


def permute_inverse(block, hot_twice):
    high = block.astype(jnp.bfloat16)
    mid = (block - high.astype(jnp.float32)).astype(jnp.bfloat16)
    return jnp.dot(jnp.concatenate([high, mid], axis=1), hot_twice, preferred_element_type=jnp.float32)


def hot_lanes(index_row):
    rows = lax.broadcasted_iota(jnp.int32, (256, 256), 0)
    return (rows == index_row).astype(jnp.float32).astype(jnp.bfloat16)


def flag_rows():
    tm = jnp.full((16,), lax.axis_index("tm"), jnp.int32)
    space = jnp.full((16,), lax.axis_index("space"), jnp.int32)
    at = jnp.arange(16, dtype=jnp.int32)
    core, z_high = tm & 1, (tm >> 1) & 3
    from_core = 1 - (at & 1)
    source = ((at >> 1) - from_core) & 3
    slot = ((z_high - source) & 3) + jnp.where(from_core != core, 4, 0)
    rest = [tm & 7, 1 - core, 1 - (space & 1), tm == 0, tm < 8, tm == 31]
    for i, value in enumerate(rest):
        slot = jnp.where(at == 8 + i, value.astype(jnp.int32), slot)
    return slot, jnp.broadcast_to(slot[:, None], (16, 128))


def layer_order(neighbours, rims):
    parts = jnp.concatenate([neighbours >> 4, neighbours & 15], axis=0).astype(jnp.float32).astype(jnp.bfloat16)
    element = lax.broadcasted_iota(jnp.int32, (256, 64), 0)
    row_at = lax.broadcasted_iota(jnp.int32, (64, 64), 0)
    lane_at = lax.broadcasted_iota(jnp.int32, (64, 64), 1)
    orders, besides = [], []
    row = rims[0:1]
    for layer in range(4):
        hot = (element == row).astype(jnp.float32).astype(jnp.bfloat16)
        found = jnp.dot(parts, hot, preferred_element_type=jnp.float32)
        found = (found[0:6] * 16 + found[6:12]).astype(jnp.int32)
        column = jnp.sum(jnp.where(row_at == lane_at, row, 0), axis=1, keepdims=True)
        local = [
            jnp.sum(jnp.where(column == found[f : f + 1], row_at, 0), axis=0, keepdims=True) + 64 * (layer & 1)
            for f in range(2, 6)
        ]
        orders.append(row)
        besides.append(jnp.concatenate(local, axis=0))
        row = rims[1:2] if layer == 2 else found[1:2]
    return jnp.concatenate(orders, axis=1), jnp.concatenate(besides, axis=1).astype(jnp.float32)


def two_tiles(ref, block):
    ref[0] = block[:, 0:128]
    ref[1] = block[:, 128:256]


def start_body(
    spread_ref, order_ref, beside_ref, states_hbm, initial_hbm, source_hbm, mass_hbm, coef_hbm, inv_hbm,
    start_ref, initial_out_ref, src_ref, own_ref, up_ref, down_ref, inv_ref, pair_ref, cross_ref,
    states_ref, initial_ref, source_ref, mass_ref, coef_ref, block_ref, sems,
):
    small = [
        (mass_hbm, mass_ref), (coef_hbm, coef_ref), (states_hbm, states_ref), (initial_hbm, initial_ref),
        (source_hbm, source_ref),
    ]
    copies = [pltpu.make_async_copy(a, b, sems.at[i]) for i, (a, b) in enumerate(small)]
    blocks = [
        pltpu.make_async_copy(inv_hbm.at[8 * i : 8 * i + 8], block_ref.at[8 * i : 8 * i + 8], sems.at[5 + i])
        for i in range(8)
    ]
    for copy in copies + blocks:
        copy.start()
    beside = beside_ref[...]
    hot = hot_lanes(order_ref[...])
    hot_twice = jnp.concatenate([hot, hot], axis=0)
    for copy in copies:
        copy.wait()
    two_tiles(start_ref, permute_lanes(states_ref[0], hot))
    two_tiles(initial_out_ref, permute_lanes(initial_ref[...], hot))
    up_ref[0:64] = start_ref[1]
    down_ref[0:64] = start_ref[0]
    for k in range(4):
        src = permute_lanes(source_ref[k], hot)
        src_ref[k, 0] = src[:, 0:128]
        src_ref[k, 1] = src[:, 128:256]
        if k % 2 == 0:
            up_ref[64 + 8 * k : 80 + 8 * k] = src[48:64, 128:256]
            down_ref[64 + 8 * k : 80 + 8 * k] = src[0:16, 0:128]
    table = jnp.concatenate(
        [
            permute_lanes(mass_ref[...], hot),
            permute_lanes(jnp.concatenate([coef_ref[...], jnp.zeros((2, 256), jnp.float32)], axis=0), hot)[0:6],
            beside,
            jnp.zeros((6, 256), jnp.float32),
        ],
        axis=0,
    )
    own_ref[...] = table

    def turn(i, carry):
        at = pl.ds(pl.multiple_of(8 * i, 8), 8)
        pltpu.make_async_copy(inv_hbm.at[at], block_ref.at[at], sems.at[5 + i]).wait()
        inv_ref[at] = permute_inverse(block_ref[at].reshape(512, 256), hot_twice).reshape(8, 64, 256)
        return carry

    lax.fori_loop(0, 8, turn, 0)
    even = spread_ref[10:11] == 1

    def lanes(tile, begin):
        return inv_ref[begin : begin + 8, :, 128 * tile : 128 * tile + 128]

    first = first_half((8, 64, 128))
    up = jnp.where(first, roll_half(lanes(1, 56)), lanes(1, 48)).reshape(512, 128)
    down = jnp.where(first, lanes(0, 0), roll_half(lanes(0, 8))).reshape(512, 128)
    pair_ref[0:512] = jnp.where(even, up, down)
    cross_ref[0:512] = jnp.where(even, down, up)
    pair_ref[512:592] = jnp.where(even, table[:, 128:256], table[:, 0:128])
    cross_ref[512:592] = jnp.where(even, table[:, 0:128], table[:, 128:256])


def restore_body(index_ref, corrected_ref, middle_ref, field_ref, final_ref, kept_ref, c_ref, f_ref, r_ref):
    hot = hot_lanes(index_ref[...])

    def back(ref):
        block = jnp.concatenate([ref[0], ref[1]], axis=1)
        high = block.astype(jnp.bfloat16)
        rest = block - high.astype(jnp.float32)
        mid = rest.astype(jnp.bfloat16)
        low = (rest - mid.astype(jnp.float32)).astype(jnp.bfloat16)

        def dot(part):
            return lax.dot_general(part, hot, (((1,), (1,)), ((), ())), preferred_element_type=jnp.float32)

        return (dot(low) + dot(mid)) + dot(high)

    c_ref[0] = back(corrected_ref)
    f_ref[0] = back(middle_ref)
    f_ref[1] = back(field_ref)
    f_ref[2] = back(final_ref)
    r_ref[0] = back(kept_ref)


def coarse_body(
    flag_ref, neighbours_hbm, rims_hbm, inv_hbm, order_ref, beside_ref, out_ref, pair_ref, cross_ref,
    neighbours_ref, rims_ref, block_ref, sems,
):
    copies = [
        pltpu.make_async_copy(neighbours_hbm, neighbours_ref, sems.at[0]),
        pltpu.make_async_copy(rims_hbm, rims_ref, sems.at[1]),
    ]
    blocks = [
        pltpu.make_async_copy(inv_hbm.at[8 * i : 8 * i + 8], block_ref.at[8 * i : 8 * i + 8], sems.at[2 + i])
        for i in range(8)
    ]
    for copy in copies + blocks:
        copy.start()
    for copy in copies:
        copy.wait()
    order_ref[...], beside_ref[...] = layer_order(neighbours_ref[...], rims_ref[...])
    hot = hot_lanes(order_ref[...])
    hot_twice = jnp.concatenate([hot, hot], axis=0)

    def turn(i, carry):
        at = pl.ds(pl.multiple_of(8 * i, 8), 8)
        pltpu.make_async_copy(inv_hbm.at[at], block_ref.at[at], sems.at[2 + i]).wait()
        out_ref[at] = permute_inverse(block_ref[at].reshape(512, 256), hot_twice).reshape(8, 64, 256)
        return carry

    lax.fori_loop(0, 8, turn, 0)

    def lanes(tile, begin):
        return out_ref[begin : begin + 4, :, 128 * tile : 128 * tile + 128]

    core_0, even = flag_ref[9:10] == 1, flag_ref[10:11] == 1
    first = first_half((4, 64, 128))

    def pack(at):
        if at < 32:
            return (
                jnp.where(first, roll_half(lanes(1, 32 + at)), lanes(1, at)),
                jnp.where(first, lanes(0, at), roll_half(lanes(0, 32 + at))),
            )
        at -= 32
        return (
            jnp.where(first, lanes(1, 56 + at), roll_half(lanes(1, 48 + at))),
            jnp.where(first, roll_half(lanes(0, at)), lanes(0, 8 + at)),
        )

    for i in range(0, 20, 4):
        (up, down), (far_up, far_down) = pack(i), pack(20 + i)
        up, down = jnp.where(core_0, up, far_up), jnp.where(core_0, down, far_down)
        pair_ref[i : i + 4] = jnp.where(even, up, down)
        cross_ref[i : i + 4] = jnp.where(even, down, up)


def combine_rows(parts):
    sub = lax.broadcasted_iota(jnp.int32, (8, 128), 0)
    m4, m2, m1 = sub < 4, (sub & 3) < 2, (sub & 1) < 1
    stage = []
    for i in range(4):
        a, b = parts[i], parts[i + 4]
        stage.append(jnp.where(m4, a, b) + pltpu.roll(jnp.where(m4, b, a), 4, 0))

    def fold(a, b, mask, dist):
        other = jnp.where(mask, b, a)
        moved = jnp.where(mask, pltpu.roll(other, 8 - dist, 0), pltpu.roll(other, dist, 0))
        return jnp.where(mask, a, b) + moved

    r0 = fold(stage[0], stage[2], m2, 2)
    r1 = fold(stage[1], stage[3], m2, 2)
    return fold(r0, r1, m1, 1)


def face_rows(tile):
    sub = lax.broadcasted_iota(jnp.int32, (8, 128), 0)
    rows = []
    for a in range(4):
        even, odd = tile[16 * a : 16 * a + 8], tile[16 * a + 8 : 16 * a + 16]
        rows.append(pltpu.roll(jnp.where(sub < 4, even, odd), 4, 0))
    ends = ((sub + 1) & 3) < 2
    for a in range(4):
        even, odd = tile[16 * a : 16 * a + 8], tile[16 * a + 8 : 16 * a + 16]
        rows.append(jnp.where(ends, even, pltpu.roll(odd, 2, 0)))
    return jnp.concatenate(rows, axis=0)


def loaded_tiles(flux_mat, items, step):
    columns = []
    for tile, from_low, from_high, (mass, index, coef, ends) in items:
        moved = coef * lane_take(face_rows(tile), index)
        rows = jnp.concatenate([moved, ends[0:1] * from_low, ends[1:2] * from_high], axis=0)
        high = rows.astype(jnp.bfloat16)
        low = (rows - high.astype(jnp.float32)).astype(jnp.bfloat16)
        columns.append(jnp.concatenate([high, low], axis=0))
    both = jnp.dot(flux_mat, jnp.concatenate(columns, axis=1), preferred_element_type=jnp.float32)
    coupling = both[0:64] + both[64:128]
    return [
        item[3][0] * item[0] - step * coupling[:, 128 * m : 128 * m + 128] for m, item in enumerate(items)
    ]


def matvec_rows(block, load):
    parts = []
    for i in range(8):
        total = block[i, 0:8] * load[0:8]
        for j in range(1, 8):
            total = total + block[i, 8 * j : 8 * j + 8] * load[8 * j : 8 * j + 8]
        parts.append(total)
    return combine_rows(parts)


def march(count, step, edge, near, far, tables, mat, inv_ref, inv_full_ref, inv_near_ref, inv_far_ref, term, work_ref, done):
    first = first_half((16, 128))
    for turn in range(count):
        left = count - 1 - turn
        t1, t2 = work_ref[0], work_ref[1]
        tiles = [t1, t2, near] + ([far] if left >= 1 else []) + ([edge] if left == 2 else [])
        hi, lo = [t[0:16] for t in tiles], [t[48:64] for t in tiles]
        items = [
            (t1, roll_half(jnp.where(first, lo[0], lo[2])), roll_half(jnp.where(first, hi[1], hi[0])), tables(0)),
            (t2, roll_half(jnp.where(first, lo[1], lo[0])), roll_half(jnp.where(first, hi[2], hi[1])), tables(1)),
        ]
        if left >= 1:
            items.append(
                (near, jnp.where(first, roll_half(lo[1]), lo[3]), jnp.where(first, hi[3], roll_half(hi[0])), tables(2))
            )
        if left == 2:
            items.append((far, jnp.where(first, lo[2], lo[4]), jnp.where(first, hi[4], hi[2]), tables(3)))
        loads = loaded_tiles(mat, items, step)

        def rows_turn(group, carry):
            rows = pl.ds(pl.multiple_of(group * 8, 8), 8)
            for m in range(2):
                value = matvec_rows(inv_ref[rows, :, 128 * m : 128 * m + 128], loads[m])
                work_ref[m, rows] = value + term(turn, m, rows)
            if left == 2:
                work_ref[2, rows] = matvec_rows(inv_full_ref[rows], loads[2]) + term(turn, 2, rows)
            return carry

        lax.fori_loop(0, 8, rows_turn, 0)
        if left == 2:
            face = [matvec_rows(inv_far_ref[8 * g : 8 * g + 8], loads[3]) + term(turn, 3, slice(8 * g, 8 * g + 8)) for g in range(2)]
            far = jnp.concatenate(face + [jnp.zeros((32, 128), jnp.float32)] + face, axis=0)
            near = work_ref[2]
        elif left == 1:
            face = [matvec_rows(inv_near_ref[8 * g : 8 * g + 8], loads[2]) + term(turn, 4, slice(8 * g, 8 * g + 8)) for g in range(2)]
            near = jnp.concatenate(face + [jnp.zeros((32, 128), jnp.float32)] + face, axis=0)
        done(turn)


def table_reader(refs):
    return lambda m: tuple(ref[m] for ref in refs)


def fine_body(
    count, near_at, switch, middle, flag_ref, v_ref, low_ref, high_ref, mass_ref, index_ref, face_ref, coef_ref, mat_ref,
    inv_ref, inv_near_ref, src_ref, start_low_ref, start_high_ref, *refs
):
    if switch:
        other_ref, out_ref = refs[:2]
        here = flag_ref[11:12] == 1
        out_ref[...] = jnp.where(here, other_ref[...], v_ref[...])
        low = jnp.where(here, start_low_ref[0:64], low_ref[...])
        high = jnp.where(here, start_high_ref[0:64], high_ref[...])
        if middle:
            refs[2][...] = out_ref[...]
    else:
        out_ref = refs[-1] if not middle else refs[-2]
        out_ref[...] = v_ref[...]
        low, high = low_ref[0:64], high_ref[0:64]
    near, far = merge(low, high), merge_far(low, high)
    first = first_half((8, 128))

    def term(turn, m, rows):
        if m == 4:
            at = near_at + rows.start
            return jnp.where(first, start_high_ref[at : at + 8], start_low_ref[at : at + 8])
        return src_ref[turn, m, rows]

    def done(turn):
        if middle and not switch and turn == 0:
            refs[-1][...] = out_ref[...]

    march(
        count, step_fine, None, near, far, table_reader((mass_ref, index_ref, face_ref, coef_ref)),
        mat_ref[...], inv_ref, None, inv_near_ref, None, term, out_ref, done,
    )


def window_body(
    count, first_slot, begins, first_group, pick,
    flag_ref, v_ref, low_ref, high_ref, mass_ref, index_ref, face_ref, coef_ref, mat_ref,
    inv_ref, inv_full_ref, inv_near_ref, inv_far_ref, term_ref, *refs
):
    if pick:
        begin_ref = refs[0]
        kept_out_ref = refs[-2]
    out_ref, up_ref, down_ref = refs[-5:-2] if pick else refs[-4:-1]
    work_ref = refs[-1]
    low, high = low_ref[...], high_ref[...]
    work_ref[0], work_ref[1] = v_ref[0], v_ref[1]
    if begins:
        here = flag_ref[12:13] >= first_group
        low, high = jnp.where(here, 0.0, low), jnp.where(here, 0.0, high)
        work_ref[0:2] = jnp.where(here, 0.0, v_ref[...])
    near, far = merge(low[0:64], high[0:64]), merge_far(low[0:64], high[0:64])
    edge = jnp.concatenate([high[64:80], jnp.zeros((32, 128), jnp.float32), low[64:80]], axis=0)
    if pick:
        kept_out_ref[...] = refs[1][...] if first_slot > 0 else jnp.zeros((4, 64, 128), jnp.float32)
    first = first_half((8, 128))

    def term(turn, m, rows):
        at = first_slot + turn
        if m == 4:
            here, there = 128 + rows.start, 176 + rows.start
            return jnp.where(first, term_ref[at, here : here + 8], term_ref[at, there : there + 8])
        if m == 3:
            return term_ref[at, 192 + rows.start : 200 + rows.start]
        return term_ref[at, pl.ds(pl.multiple_of(64 * m + rows.start, 8), 8)]

    def done(turn):
        if pick:
            mine = flag_ref[8:9] == first_slot + turn
            for m in range(2):
                rows = slice(64 * m, 64 * m + 64)
                kept_out_ref[m] = jnp.where(mine, work_ref[m] + begin_ref[m], kept_out_ref[m])
                kept_out_ref[2 + m] = jnp.where(mine, term_ref[first_slot + turn, rows], kept_out_ref[2 + m])

    march(
        count, step_coarse, edge, near, far, table_reader((mass_ref, index_ref, face_ref, coef_ref)),
        mat_ref[...], inv_ref, inv_full_ref, inv_near_ref, inv_far_ref, term, work_ref, done,
    )
    out_ref[0] = work_ref[0]
    out_ref[1] = work_ref[1]
    up_ref[0:64] = work_ref[1]
    up_ref[64:80] = work_ref[0, 48:64]
    down_ref[0:64] = work_ref[0]
    down_ref[64:80] = work_ref[1, 0:16]


def term_body(flag_ref, field_ref, handed_ref, initial_ref, states_ref, out_ref):
    last = flag_ref[13:14] == 1
    out_ref[...] = jnp.where(last, initial_ref[...] - states_ref[...], field_ref[...] - handed_ref[...])


def pack_terms_body(term_ref, low_ref, high_ref, out_ref):
    low, high = low_ref[...], high_ref[...]
    out_ref[0:64] = term_ref[0]
    out_ref[64:128] = term_ref[1]
    out_ref[128:192] = merge(low, high)
    out_ref[192:208] = roll_half(jnp.where(first_half((16, 128)), low[48:64], high[0:16]))


def stack_body(a_ref, b_ref, c_ref, d_ref, out_ref):
    for i, ref in enumerate((a_ref, b_ref, c_ref, d_ref)):
        out_ref[i] = ref[...]


def flux_constants():
    left, right = np.zeros((64, 96), np.float32), np.zeros((96, 96), np.float32)
    for face in range(6):
        axis, side = divmod(face, 2)
        for k in range(16):
            p, q = divmod(k, 4)
            node = [lambda d: 16 * d + 4 * p + q, lambda d: 16 * p + 4 * d + q, lambda d: 16 * p + 4 * q + d][axis]
            left[node(3 * side), 16 * face + k] = 1
    for row in range(96):
        group, sub = divmod(row, 8)
        if row >= 64:
            face, k = divmod(row - 64, 16)
        elif row < 32:
            face, k = 2 + sub // 4, 4 * group + sub % 4
        else:
            node = 16 * (group - 4) + (sub if sub % 4 in (0, 3) else 8 + (sub - 2) % 8)
            face, k = (4 if node % 4 == 3 else 5), node // 4
        right[16 * face + k, row] = 1
    return left, right


def flux_body(mats_ref, left_ref, right_ref, out_ref):
    dot = functools.partial(jnp.dot, preferred_element_type=jnp.float32, precision=HI)
    parts = [dot(mats_ref[f], right_ref[16 * f : 16 * f + 16]) for f in range(6)]
    full = dot(left_ref[...], jnp.concatenate(parts, axis=0))
    high = full.astype(jnp.bfloat16)
    low = (full - high.astype(jnp.float32)).astype(jnp.bfloat16)
    out_ref[...] = jnp.concatenate(
        [jnp.concatenate([high, high], axis=1), jnp.concatenate([low, low], axis=1)], axis=0
    )


def tables_body(flag_ref, own_ref, pair_ref, cross_ref, inv_near_ref, mass_ref, index_ref, face_ref, coef_ref):
    row = lax.broadcasted_iota(jnp.int32, (64, 128), 0)
    along_b = row < 32
    second = jnp.where(along_b, (row >> 2) & 1, 1 - (row & 1)) == 1
    even = flag_ref[10:11] == 1

    def beside(begin, end):
        pair, cross = pair_ref[begin:end], cross_ref[begin:end]
        return jnp.where(even, cross, pair), jnp.where(even, pair, cross)

    for i in range(8):
        low, high = beside(64 * i, 64 * i + 64)
        inv_near_ref[i], inv_near_ref[8 + i] = merge(low, high), merge_far(low, high)
    low, high = beside(512, 592)
    tiles = [own_ref[0:80, 0:128], own_ref[0:80, 128:256], merge(low, high), merge_far(low, high)]
    for m, tile in enumerate(tiles):
        index = tile[70:74].astype(jnp.int32)
        if m == 3:
            index = (index + 64) & 127

        def spread(rows):
            return jnp.where(along_b, jnp.where(second, rows[1:2], rows[0:1]), jnp.where(second, rows[3:4], rows[2:3]))

        mass_ref[m] = tile[0:64]
        coef_ref[m] = tile[64:72]
        index_ref[m] = spread(index)
        face_ref[m] = spread(tile[66:70])


def sort_terms_body(flag_ref, own_ref, other_ref, out_ref):
    for j in range(8):
        slot = flag_ref[j]

        @pl.when(slot < 4)
        def _():
            out_ref[j] = own_ref[slot & 3]

        @pl.when(slot >= 4)
        def _():
            out_ref[j] = other_ref[slot & 3]


def join_halo_body(*refs):
    out_ref = refs[-1]
    out_ref[0] = refs[0][...]
    out_ref[1] = refs[1][...]


def halo_body(flag_ref, own_ref, other_ref, near_ref, full_ref, far_ref):
    core_0, even = flag_ref[9:10] == 1, flag_ref[10:11] == 1
    first = first_half((4, 64, 128))
    for part in range(2):
        for i in range(0, 20, 4):
            rows = slice(i, i + 4)
            mine, others = (own_ref[0, rows], own_ref[1, rows]), (other_ref[0, rows], other_ref[1, rows])
            yes, no = (mine, others) if part == 0 else (others, mine)
            pair, cross = jnp.where(core_0, yes[0], no[0]), jnp.where(core_0, yes[1], no[1])
            low, high = jnp.where(even, cross, pair), jnp.where(even, pair, cross)
            at = 20 * part + i
            a, b = merge(low, high), merge_far(low, high)
            if at < 32:
                full_ref[at : at + 4], full_ref[32 + at : 36 + at] = a, b
            else:
                far_ref[at - 32 : at - 28], far_ref[at - 24 : at - 20] = a, b
    for i in range(0, 16, 4):
        near_ref[i : i + 4] = jnp.where(first, full_ref[i : i + 4], full_ref[48 + i : 52 + i])


def per_device(
    states, initial, source, mass, inv_fine, inv_coarse, face_mats, face_coef, neighbours, rims
):
    flags, spread = flag_rows()
    pair = f32(2, 64, 128)

    def from_hbm(body, out_shapes, held, inputs, copies, cost):
        hbm = pl.BlockSpec(memory_space=pltpu.HBM)
        scratch = [pltpu.VMEM(a.shape, a.dtype) for a in inputs] + [pltpu.SemaphoreType.DMA((copies,))]
        return call(
            body, out_shapes, *held, *(pltpu.with_memory_space_constraint(a, pltpu.HBM) for a in inputs),
            specs=[VM] * len(held) + [hbm] * len(inputs), scratch=scratch, mib=20, cost=cost,
        )

    cost = pl.CostEstimate(flops=4 << 30, bytes_accessed=16 << 20, transcendentals=0)
    order_row, beside, inv_c, coarse_pair, coarse_cross = from_hbm(
        coarse_body,
        [
            jax.ShapeDtypeStruct((1, 256), jnp.int32), f32(4, 256), vmem_f32(64, 64, 256),
            f32(20, 64, 128), f32(20, 64, 128),
        ],
        [spread], (neighbours, rims, inv_coarse), 10, cost,
    )
    got_coarse = send(coarse_pair, HALO_PAIR), send(coarse_cross, HALO_CROSS)
    start, first_value, src, table, up_start, down_start, inv_f, fine_pair, fine_cross = from_hbm(
        start_body,
        [
            pair, pair, f32(4, 2, 64, 128), f32(80, 256), f32(96, 128), f32(96, 128), vmem_f32(64, 64, 256),
            f32(592, 128), f32(592, 128),
        ],
        [spread, order_row, beside], (states, initial, source, mass, face_coef, inv_fine), 13, cost,
    )
    got_coarse_pair, got_coarse_cross = got_coarse
    up_start, down_start, fine_pair, fine_cross, start, got_coarse_pair = lax.optimization_barrier(
        (up_start, down_start, fine_pair, fine_cross, start, got_coarse_pair)
    )
    low_start, high_start = send(up_start, UP), send(down_start, DOWN)
    got_pair, got_cross = send(fine_pair, HALO_PAIR), send(fine_cross, HALO_CROSS)
    far_start = send(start, FIRST_TO_LAST)
    low_start, high_start, got_pair, got_cross, far_start, got_coarse_cross = lax.optimization_barrier(
        (low_start, high_start, got_pair, got_cross, far_start, got_coarse_cross)
    )
    got_coarse = got_coarse_pair, got_coarse_cross
    fine_near, *tables = call(
        tables_body,
        [
            vmem_f32(16, 64, 128), f32(4, 64, 128), jax.ShapeDtypeStruct((4, 64, 128), jnp.int32), f32(4, 64, 128),
            f32(4, 8, 128),
        ],
        spread, table, got_pair, got_cross,
    )
    left, right = flux_constants()
    mat = call(
        flux_body, [jax.ShapeDtypeStruct((128, 192), jnp.bfloat16)], face_mats, jnp.asarray(left), jnp.asarray(right)
    )[0]

    def fine_march(field, low, high, at, count, other=(), middle=False):
        operands = (
            spread, field, low, high, *tables, mat, pinned(inv_f), fine_near, src[at : at + count],
            low_start, high_start, *other,
        )
        return call(
            functools.partial(fine_body, count, 64 + 8 * at, bool(other), middle), [pair] * (2 if middle else 1),
            *operands,
        )

    def exchange(field):
        return send(field[1], UP), send(field[0], DOWN)

    (field,) = fine_march(start, low_start, high_start, 0, 2)
    low, high = exchange(field)
    (handed,) = fine_march(field, low, high, 2, 2)
    arrived, low, high = send(handed, SLICE), send(handed[1], SLICE_UP), send(handed[0], SLICE_DOWN)

    field, begin = fine_march(arrived, low, high, 0, 2, (start,), middle=True)
    low, high = exchange(field)
    (field,) = fine_march(field, low, high, 2, 2)
    next_term = call(term_body, [pair], spread, field, handed, first_value, far_start)[0]

    joined = call(join_halo_body, [f32(2, 20, 64, 128)], *got_coarse)[0]
    inv_near, inv_full, inv_far = call(
        halo_body, [vmem_f32(16, 64, 128), vmem_f32(64, 64, 128), vmem_f32(16, 64, 128)],
        spread, joined, send(joined, CORE),
    )
    packed = call(pack_terms_body, [f32(208, 128)], next_term, *exchange(next_term))[0]
    terms = call(stack_body, [f32(4, 208, 128)], *(send(packed, pairs) for pairs in GROUP))[0]
    terms = call(sort_terms_body, [f32(8, 208, 128)], flags, terms, send(terms, CORE), specs=[SM, VM, VM])[0]

    value, up, down = next_term, low_start, high_start
    picked = []
    for turn in range(4):
        last = turn == 3
        for at, count in ((0, 3), (3, 3), (6, 2)):
            if at > 0:
                low, high = send(up, UP), send(down, DOWN)
            elif turn > 0:
                value, low, high = send(value, YNEXT), send(up, Y_UP), send(down, Y_DOWN)
            else:
                low, high = up, down
            value, up, down, *picked = call(
                functools.partial(window_body, count, at, at == 0, 0 if turn == 0 else 1, last),
                [pair, f32(80, 128), f32(80, 128)] + [f32(4, 64, 128)] * last,
                spread, value, low, high, *tables, mat,
                pinned(inv_c), pinned(inv_full), pinned(inv_near), pinned(inv_far), pinned(terms),
                *([begin] * last), *picked, scratch=[pltpu.VMEM((3, 64, 128), jnp.float32)],
            )
    kept = picked[0]

    corrected = kept[0:2]
    low, high = exchange(corrected)
    field, middle = fine_march(corrected, low, high, 0, 2, middle=True)
    low, high = exchange(field)
    (final,) = fine_march(field, low, high, 2, 1)
    return call(
        restore_body, [f32(1, 64, 256), f32(3, 64, 256), f32(1, 64, 256)],
        order_row, corrected, middle, field, final, kept[2:4],
    )


def solution(mesh):
    return jax.shard_map(
        per_device,
        mesh=mesh,
        in_specs=(
            P("tm", None, "space"),
            P(None, "space"),
            P("tm", None, "space"),
            P(None, "space"),
            P(None, None, "space"),
            P(None, None, "space"),
            P(),
            P(None, "space"),
            P(None, "space"),
            P(None, "space"),
        ),
        out_specs=(P("tm", None, "space"), P("tm", None, "space"), P("tm", None, "space")),
        check_vma=False,
    )
```

```python
import functools

import jax
import jax.numpy as jnp
import numpy as np
from jax import lax
from jax.experimental import pallas as pl
from jax.experimental.pallas import tpu as pltpu
from jax.sharding import PartitionSpec as P

step_fine = 0.1
step_coarse = 0.25
AXES = ("tm", "space")
VM = pl.BlockSpec(memory_space=pltpu.VMEM)
SM = pl.BlockSpec(memory_space=pltpu.SMEM)
HI = lax.Precision.HIGHEST


def device_index(x, y, z, core):
    x, y, z = x % 4, y % 4, z % 8
    return (y * 8 + (z // 2) * 2 + core) * 8 + x * 2 + z % 2


def pairs_of(rule):
    out = []
    for x in range(4):
        for y in range(4):
            for z in range(8):
                for core in range(2):
                    out.append((device_index(x, y, z, core), device_index(*rule(x, y, z, core))))
    return out


def space_up(x, y, z, core):
    return (x, y, z + 1, core) if z % 2 == 0 else (x + 1, y, z - 1, core)


def space_down(x, y, z, core):
    return (x, y, z - 1, core) if z % 2 == 1 else (x - 1, y, z + 1, core)


def next_slice(x, y, z, core):
    zh, zl = z // 2, z % 2
    t = (y * 8 + zh * 2 + core + 1) % 32
    return (x, t // 8, (t % 8) // 2 * 2 + zl, t % 2)


def then(first, second):
    return lambda x, y, z, core: second(*first(x, y, z, core))


def next_y(x, y, z, core):
    return (x, y + 1, z, core)


def halo_pair(x, y, z, core):
    way = 1 if (z % 2 == 0) == (core == 0) else -1
    return (x, y, z + way, core)


def halo_cross(x, y, z, core):
    way = 1 if (z % 2 == 0) == (core == 0) else -1
    return (x + (1 if z % 2 == 1 else -1), y, z + way, core)


def other_core(x, y, z, core):
    return (x, y, z, 1 - core)


UP, DOWN = pairs_of(space_up), pairs_of(space_down)
SLICE = pairs_of(next_slice)
SLICE_UP, SLICE_DOWN = pairs_of(then(next_slice, space_up)), pairs_of(then(next_slice, space_down))
YNEXT = pairs_of(next_y)
Y_UP, Y_DOWN = pairs_of(then(next_y, space_up)), pairs_of(then(next_y, space_down))
HALO_PAIR, HALO_CROSS = pairs_of(halo_pair), pairs_of(halo_cross)
CORE = pairs_of(other_core)
def group_pairs(far):
    def rule(x, y, z, core):
        return (x, y + 1 if core == 1 and z // 2 == 3 else y, z + 2 * far, core)

    return pairs_of(rule)


GROUP = [group_pairs(far) for far in range(4)]
FIRST_TO_LAST = [(device_index(x, 0, z, 0), device_index(x, 3, 6 + z, 1)) for x in range(4) for z in range(2)]


def send(array, pairs):
    return lax.ppermute(array, AXES, pairs)


def f32(*shape):
    return jax.ShapeDtypeStruct(shape, jnp.float32)


def vmem_f32(*shape):
    return pltpu.VMEM(shape, jnp.float32)


def pinned(array):
    return pltpu.with_memory_space_constraint(array, pltpu.VMEM)


def call(body, out_shapes, *args, specs=None, mib=8, scratch=(), cost=None):
    return pl.pallas_call(
        body,
        out_shape=out_shapes,
        in_specs=specs or [VM] * len(args),
        out_specs=[VM] * len(out_shapes),
        scratch_shapes=list(scratch),
        compiler_params=pltpu.CompilerParams(vmem_limit_bytes=mib << 20),
        cost_estimate=cost,
    )(*args)


def first_half(shape):
    return lax.broadcasted_iota(jnp.int32, shape, len(shape) - 1) < 64


def roll_half(block):
    return pltpu.roll(block, 64, block.ndim - 1)


def merge(low, high):
    return jnp.where(first_half(low.shape), high, low)


def merge_far(low, high):
    return roll_half(jnp.where(first_half(low.shape), low, high))


def lane_take(block, index):
    return jnp.take_along_axis(block, index, axis=1, mode="promise_in_bounds")


def permute_lanes(block, hot):
    high = block.astype(jnp.bfloat16)
    rest = block - high.astype(jnp.float32)
    mid = rest.astype(jnp.bfloat16)
    low = (rest - mid.astype(jnp.float32)).astype(jnp.bfloat16)
    dot = functools.partial(jnp.dot, preferred_element_type=jnp.float32)
    return (dot(low, hot) + dot(mid, hot)) + dot(high, hot)


def permute_inverse(block, hot_twice):
    high = block.astype(jnp.bfloat16)
    mid = (block - high.astype(jnp.float32)).astype(jnp.bfloat16)
    return jnp.dot(jnp.concatenate([high, mid], axis=1), hot_twice, preferred_element_type=jnp.float32)


def hot_lanes(index_row):
    rows = lax.broadcasted_iota(jnp.int32, (256, 256), 0)
    return (rows == index_row).astype(jnp.float32).astype(jnp.bfloat16)


def flag_rows():
    tm = jnp.full((16,), lax.axis_index("tm"), jnp.int32)
    space = jnp.full((16,), lax.axis_index("space"), jnp.int32)
    at = jnp.arange(16, dtype=jnp.int32)
    core, z_high = tm & 1, (tm >> 1) & 3
    from_core = 1 - (at & 1)
    source = ((at >> 1) - from_core) & 3
    slot = ((z_high - source) & 3) + jnp.where(from_core != core, 4, 0)
    rest = [tm & 7, 1 - core, 1 - (space & 1), tm == 0, tm < 8, tm == 31]
    for i, value in enumerate(rest):
        slot = jnp.where(at == 8 + i, value.astype(jnp.int32), slot)
    return slot, jnp.broadcast_to(slot[:, None], (16, 128))


def layer_order(neighbours, rims):
    parts = jnp.concatenate([neighbours >> 4, neighbours & 15], axis=0).astype(jnp.float32).astype(jnp.bfloat16)
    element = lax.broadcasted_iota(jnp.int32, (256, 64), 0)
    row_at = lax.broadcasted_iota(jnp.int32, (64, 64), 0)
    lane_at = lax.broadcasted_iota(jnp.int32, (64, 64), 1)
    orders, besides = [], []
    row = rims[0:1]
    for layer in range(4):
        hot = (element == row).astype(jnp.float32).astype(jnp.bfloat16)
        found = jnp.dot(parts, hot, preferred_element_type=jnp.float32)
        found = (found[0:6] * 16 + found[6:12]).astype(jnp.int32)
        column = jnp.sum(jnp.where(row_at == lane_at, row, 0), axis=1, keepdims=True)
        local = [
            jnp.sum(jnp.where(column == found[f : f + 1], row_at, 0), axis=0, keepdims=True) + 64 * (layer & 1)
            for f in range(2, 6)
        ]
        orders.append(row)
        besides.append(jnp.concatenate(local, axis=0))
        row = rims[1:2] if layer == 2 else found[1:2]
    return jnp.concatenate(orders, axis=1), jnp.concatenate(besides, axis=1).astype(jnp.float32)


def two_tiles(ref, block):
    ref[0] = block[:, 0:128]
    ref[1] = block[:, 128:256]


def start_body(
    spread_ref, order_ref, beside_ref, states_hbm, initial_hbm, source_hbm, mass_hbm, coef_hbm, inv_hbm,
    start_ref, initial_out_ref, src_ref, own_ref, up_ref, down_ref, inv_ref, pair_ref, cross_ref,
    states_ref, initial_ref, source_ref, mass_ref, coef_ref, block_ref, sems,
):
    small = [
        (mass_hbm, mass_ref), (coef_hbm, coef_ref), (states_hbm, states_ref), (initial_hbm, initial_ref),
        (source_hbm, source_ref),
    ]
    copies = [pltpu.make_async_copy(a, b, sems.at[i]) for i, (a, b) in enumerate(small)]
    blocks = [
        pltpu.make_async_copy(inv_hbm.at[8 * i : 8 * i + 8], block_ref.at[8 * i : 8 * i + 8], sems.at[5 + i])
        for i in range(8)
    ]
    for copy in copies + blocks:
        copy.start()
    beside = beside_ref[...]
    hot = hot_lanes(order_ref[...])
    hot_twice = jnp.concatenate([hot, hot], axis=0)
    for copy in copies:
        copy.wait()
    two_tiles(start_ref, permute_lanes(states_ref[0], hot))
    two_tiles(initial_out_ref, permute_lanes(initial_ref[...], hot))
    up_ref[0:64] = start_ref[1]
    down_ref[0:64] = start_ref[0]
    for k in range(4):
        src = permute_lanes(source_ref[k], hot)
        src_ref[k, 0] = src[:, 0:128]
        src_ref[k, 1] = src[:, 128:256]
        if k % 2 == 0:
            up_ref[64 + 8 * k : 80 + 8 * k] = src[48:64, 128:256]
            down_ref[64 + 8 * k : 80 + 8 * k] = src[0:16, 0:128]
    table = jnp.concatenate(
        [
            permute_lanes(mass_ref[...], hot),
            permute_lanes(jnp.concatenate([coef_ref[...], jnp.zeros((2, 256), jnp.float32)], axis=0), hot)[0:6],
            beside,
            jnp.zeros((6, 256), jnp.float32),
        ],
        axis=0,
    )
    own_ref[...] = table

    def turn(i, carry):
        at = pl.ds(pl.multiple_of(8 * i, 8), 8)
        pltpu.make_async_copy(inv_hbm.at[at], block_ref.at[at], sems.at[5 + i]).wait()
        inv_ref[at] = permute_inverse(block_ref[at].reshape(512, 256), hot_twice).reshape(8, 64, 256)
        return carry

    lax.fori_loop(0, 8, turn, 0)
    even = spread_ref[10:11] == 1

    def lanes(tile, begin):
        return inv_ref[begin : begin + 8, :, 128 * tile : 128 * tile + 128]

    first = first_half((8, 64, 128))
    up = jnp.where(first, roll_half(lanes(1, 56)), lanes(1, 48)).reshape(512, 128)
    down = jnp.where(first, lanes(0, 0), roll_half(lanes(0, 8))).reshape(512, 128)
    pair_ref[0:512] = jnp.where(even, up, down)
    cross_ref[0:512] = jnp.where(even, down, up)
    pair_ref[512:592] = jnp.where(even, table[:, 128:256], table[:, 0:128])
    cross_ref[512:592] = jnp.where(even, table[:, 0:128], table[:, 128:256])


def restored(blocks, index_row):
    hot = hot_lanes(index_row)
    block = jnp.concatenate([jnp.concatenate([b[0], b[1]], axis=1) for b in blocks], axis=0)
    rows = block.shape[0]
    high = block.astype(jnp.bfloat16)
    rest = block - high.astype(jnp.float32)
    mid = rest.astype(jnp.bfloat16)
    low = (rest - mid.astype(jnp.float32)).astype(jnp.bfloat16)
    out = lax.dot_general(
        jnp.concatenate([high, mid, low], axis=0), hot, (((1,), (1,)), ((), ())), preferred_element_type=jnp.float32
    )
    return (out[2 * rows :] + out[rows : 2 * rows]) + out[:rows]


def restore_body(index_ref, corrected_ref, middle_ref, field_ref, kept_ref, c_ref, r_ref, f_ref):
    out = restored([r[...] for r in (corrected_ref, kept_ref, middle_ref, field_ref)], index_ref[...])
    c_ref[0] = out[0:64]
    r_ref[0] = out[64:128]
    f_ref[0] = out[128:192]
    f_ref[1] = out[192:256]


def restore_last_body(index_ref, final_ref, others_ref, f_ref):
    f_ref[0] = others_ref[0]
    f_ref[1] = others_ref[1]
    f_ref[2] = restored([final_ref[...]], index_ref[...])


def coarse_body(
    flag_ref, neighbours_hbm, rims_hbm, inv_hbm, order_ref, beside_ref, out_ref, pair_ref, cross_ref,
    neighbours_ref, rims_ref, block_ref, sems,
):
    copies = [
        pltpu.make_async_copy(neighbours_hbm, neighbours_ref, sems.at[0]),
        pltpu.make_async_copy(rims_hbm, rims_ref, sems.at[1]),
    ]
    blocks = [
        pltpu.make_async_copy(inv_hbm.at[8 * i : 8 * i + 8], block_ref.at[8 * i : 8 * i + 8], sems.at[2 + i])
        for i in range(8)
    ]
    for copy in copies + blocks:
        copy.start()
    for copy in copies:
        copy.wait()
    order_ref[...], beside_ref[...] = layer_order(neighbours_ref[...], rims_ref[...])
    hot = hot_lanes(order_ref[...])
    hot_twice = jnp.concatenate([hot, hot], axis=0)

    def turn(i, carry):
        at = pl.ds(pl.multiple_of(8 * i, 8), 8)
        pltpu.make_async_copy(inv_hbm.at[at], block_ref.at[at], sems.at[2 + i]).wait()
        out_ref[at] = permute_inverse(block_ref[at].reshape(512, 256), hot_twice).reshape(8, 64, 256)
        return carry

    lax.fori_loop(0, 8, turn, 0)

    def lanes(tile, begin):
        return out_ref[begin : begin + 4, :, 128 * tile : 128 * tile + 128]

    core_0, even = flag_ref[9:10] == 1, flag_ref[10:11] == 1
    first = first_half((4, 64, 128))

    def pack(at):
        if at < 32:
            return (
                jnp.where(first, roll_half(lanes(1, 32 + at)), lanes(1, at)),
                jnp.where(first, lanes(0, at), roll_half(lanes(0, 32 + at))),
            )
        at -= 32
        return (
            jnp.where(first, lanes(1, 56 + at), roll_half(lanes(1, 48 + at))),
            jnp.where(first, roll_half(lanes(0, at)), lanes(0, 8 + at)),
        )

    for i in range(0, 20, 4):
        (up, down), (far_up, far_down) = pack(i), pack(20 + i)
        up, down = jnp.where(core_0, up, far_up), jnp.where(core_0, down, far_down)
        pair_ref[i : i + 4] = jnp.where(even, up, down)
        cross_ref[i : i + 4] = jnp.where(even, down, up)


def combine_rows(parts):
    sub = lax.broadcasted_iota(jnp.int32, (8, 128), 0)
    m4, m2, m1 = sub < 4, (sub & 3) < 2, (sub & 1) < 1
    stage = []
    for i in range(4):
        a, b = parts[i], parts[i + 4]
        stage.append(jnp.where(m4, a, b) + pltpu.roll(jnp.where(m4, b, a), 4, 0))

    def fold(a, b, mask, dist):
        other = jnp.where(mask, b, a)
        moved = jnp.where(mask, pltpu.roll(other, 8 - dist, 0), pltpu.roll(other, dist, 0))
        return jnp.where(mask, a, b) + moved

    r0 = fold(stage[0], stage[2], m2, 2)
    r1 = fold(stage[1], stage[3], m2, 2)
    return fold(r0, r1, m1, 1)


def face_rows(tile):
    sub = lax.broadcasted_iota(jnp.int32, (8, 128), 0)
    rows = []
    for a in range(4):
        even, odd = tile[16 * a : 16 * a + 8], tile[16 * a + 8 : 16 * a + 16]
        rows.append(pltpu.roll(jnp.where(sub < 4, even, odd), 4, 0))
    ends = ((sub + 1) & 3) < 2
    for a in range(4):
        even, odd = tile[16 * a : 16 * a + 8], tile[16 * a + 8 : 16 * a + 16]
        rows.append(jnp.where(ends, even, pltpu.roll(odd, 2, 0)))
    return jnp.concatenate(rows, axis=0)


def loaded_tiles(flux_mat, items, step):
    columns = []
    for tile, from_low, from_high, (mass, index, coef, ends) in items:
        moved = coef * lane_take(face_rows(tile), index)
        rows = jnp.concatenate([moved, ends[0:1] * from_low, ends[1:2] * from_high], axis=0)
        high = rows.astype(jnp.bfloat16)
        low = (rows - high.astype(jnp.float32)).astype(jnp.bfloat16)
        columns.append(jnp.concatenate([high, low], axis=0))
    both = jnp.dot(flux_mat, jnp.concatenate(columns, axis=1), preferred_element_type=jnp.float32)
    coupling = both[0:64] + both[64:128]
    return [
        item[3][0] * item[0] - step * coupling[:, 128 * m : 128 * m + 128] for m, item in enumerate(items)
    ]


def matvec_rows(block, load):
    parts = []
    for i in range(8):
        total = block[i, 0:8] * load[0:8]
        for j in range(1, 8):
            total = total + block[i, 8 * j : 8 * j + 8] * load[8 * j : 8 * j + 8]
        parts.append(total)
    return combine_rows(parts)


def march(count, step, edge, near, far, tables, mat, inv_ref, inv_full_ref, inv_near_ref, inv_far_ref, term, work_ref, done):
    first = first_half((16, 128))
    for turn in range(count):
        left = count - 1 - turn
        t1, t2 = work_ref[0], work_ref[1]
        tiles = [t1, t2, near] + ([far] if left >= 1 else []) + ([edge] if left == 2 else [])
        hi, lo = [t[0:16] for t in tiles], [t[48:64] for t in tiles]
        items = [
            (t1, roll_half(jnp.where(first, lo[0], lo[2])), roll_half(jnp.where(first, hi[1], hi[0])), tables(0)),
            (t2, roll_half(jnp.where(first, lo[1], lo[0])), roll_half(jnp.where(first, hi[2], hi[1])), tables(1)),
        ]
        if left >= 1:
            items.append(
                (near, jnp.where(first, roll_half(lo[1]), lo[3]), jnp.where(first, hi[3], roll_half(hi[0])), tables(2))
            )
        if left == 2:
            items.append((far, jnp.where(first, lo[2], lo[4]), jnp.where(first, hi[4], hi[2]), tables(3)))
        loads = loaded_tiles(mat, items, step)

        def rows_turn(group, carry):
            rows = pl.ds(pl.multiple_of(group * 8, 8), 8)
            for m in range(2):
                value = matvec_rows(inv_ref[rows, :, 128 * m : 128 * m + 128], loads[m])
                work_ref[m, rows] = value + term(turn, m, rows)
            if left == 2:
                work_ref[2, rows] = matvec_rows(inv_full_ref[rows], loads[2]) + term(turn, 2, rows)
            return carry

        lax.fori_loop(0, 8, rows_turn, 0)
        if left == 2:
            face = [matvec_rows(inv_far_ref[8 * g : 8 * g + 8], loads[3]) + term(turn, 3, slice(8 * g, 8 * g + 8)) for g in range(2)]
            far = jnp.concatenate(face + [jnp.zeros((32, 128), jnp.float32)] + face, axis=0)
            near = work_ref[2]
        elif left == 1:
            face = [matvec_rows(inv_near_ref[8 * g : 8 * g + 8], loads[2]) + term(turn, 4, slice(8 * g, 8 * g + 8)) for g in range(2)]
            near = jnp.concatenate(face + [jnp.zeros((32, 128), jnp.float32)] + face, axis=0)
        done(turn)


def table_reader(refs):
    return lambda m: tuple(ref[m] for ref in refs)


def fine_body(
    count, near_at, switch, middle, flag_ref, v_ref, low_ref, high_ref, mass_ref, index_ref, face_ref, coef_ref, mat_ref,
    inv_ref, inv_near_ref, src_ref, start_low_ref, start_high_ref, *refs
):
    if switch:
        other_ref, out_ref = refs[:2]
        here = flag_ref[11:12] == 1
        out_ref[...] = jnp.where(here, other_ref[...], v_ref[...])
        low = jnp.where(here, start_low_ref[0:64], low_ref[...])
        high = jnp.where(here, start_high_ref[0:64], high_ref[...])
        if middle:
            refs[2][...] = out_ref[...]
    else:
        out_ref = refs[-1] if not middle else refs[-2]
        out_ref[...] = v_ref[...]
        low, high = low_ref[0:64], high_ref[0:64]
    near, far = merge(low, high), merge_far(low, high)
    first = first_half((8, 128))

    def term(turn, m, rows):
        if m == 4:
            at = near_at + rows.start
            return jnp.where(first, start_high_ref[at : at + 8], start_low_ref[at : at + 8])
        return src_ref[turn, m, rows]

    def done(turn):
        if middle and not switch and turn == 0:
            refs[-1][...] = out_ref[...]

    march(
        count, step_fine, None, near, far, table_reader((mass_ref, index_ref, face_ref, coef_ref)),
        mat_ref[...], inv_ref, None, inv_near_ref, None, term, out_ref, done,
    )


def window_body(
    count, first_slot, begins, first_group, pick,
    flag_ref, v_ref, low_ref, high_ref, mass_ref, index_ref, face_ref, coef_ref, mat_ref,
    inv_ref, inv_full_ref, inv_near_ref, inv_far_ref, term_ref, *refs
):
    if pick:
        begin_ref = refs[0]
        kept_out_ref = refs[-2]
    out_ref, up_ref, down_ref = refs[-5:-2] if pick else refs[-4:-1]
    work_ref = refs[-1]
    low, high = low_ref[...], high_ref[...]
    work_ref[0], work_ref[1] = v_ref[0], v_ref[1]
    if begins:
        here = flag_ref[12:13] >= first_group
        low, high = jnp.where(here, 0.0, low), jnp.where(here, 0.0, high)
        work_ref[0:2] = jnp.where(here, 0.0, v_ref[...])
    near, far = merge(low[0:64], high[0:64]), merge_far(low[0:64], high[0:64])
    edge = jnp.concatenate([high[64:80], jnp.zeros((32, 128), jnp.float32), low[64:80]], axis=0)
    if pick:
        kept_out_ref[...] = refs[1][...] if first_slot > 0 else jnp.zeros((4, 64, 128), jnp.float32)
    first = first_half((8, 128))

    def term(turn, m, rows):
        at = first_slot + turn
        if m == 4:
            here, there = 128 + rows.start, 176 + rows.start
            return jnp.where(first, term_ref[at, here : here + 8], term_ref[at, there : there + 8])
        if m == 3:
            return term_ref[at, 192 + rows.start : 200 + rows.start]
        return term_ref[at, pl.ds(pl.multiple_of(64 * m + rows.start, 8), 8)]

    def done(turn):
        if pick:
            mine = flag_ref[8:9] == first_slot + turn
            for m in range(2):
                rows = slice(64 * m, 64 * m + 64)
                kept_out_ref[m] = jnp.where(mine, work_ref[m] + begin_ref[m], kept_out_ref[m])
                kept_out_ref[2 + m] = jnp.where(mine, term_ref[first_slot + turn, rows], kept_out_ref[2 + m])

    march(
        count, step_coarse, edge, near, far, table_reader((mass_ref, index_ref, face_ref, coef_ref)),
        mat_ref[...], inv_ref, inv_full_ref, inv_near_ref, inv_far_ref, term, work_ref, done,
    )
    out_ref[0] = work_ref[0]
    out_ref[1] = work_ref[1]
    up_ref[0:64] = work_ref[1]
    up_ref[64:80] = work_ref[0, 48:64]
    down_ref[0:64] = work_ref[0]
    down_ref[64:80] = work_ref[1, 0:16]


def term_body(flag_ref, field_ref, handed_ref, initial_ref, states_ref, out_ref):
    last = flag_ref[13:14] == 1
    out_ref[...] = jnp.where(last, initial_ref[...] - states_ref[...], field_ref[...] - handed_ref[...])


def pack_terms_body(term_ref, low_ref, high_ref, out_ref):
    low, high = low_ref[...], high_ref[...]
    out_ref[0:64] = term_ref[0]
    out_ref[64:128] = term_ref[1]
    out_ref[128:192] = merge(low, high)
    out_ref[192:208] = roll_half(jnp.where(first_half((16, 128)), low[48:64], high[0:16]))


def stack_body(a_ref, b_ref, c_ref, d_ref, out_ref):
    for i, ref in enumerate((a_ref, b_ref, c_ref, d_ref)):
        out_ref[i] = ref[...]


def flux_constants():
    left, right = np.zeros((64, 96), np.float32), np.zeros((96, 96), np.float32)
    for face in range(6):
        axis, side = divmod(face, 2)
        for k in range(16):
            p, q = divmod(k, 4)
            node = [lambda d: 16 * d + 4 * p + q, lambda d: 16 * p + 4 * d + q, lambda d: 16 * p + 4 * q + d][axis]
            left[node(3 * side), 16 * face + k] = 1
    for row in range(96):
        group, sub = divmod(row, 8)
        if row >= 64:
            face, k = divmod(row - 64, 16)
        elif row < 32:
            face, k = 2 + sub // 4, 4 * group + sub % 4
        else:
            node = 16 * (group - 4) + (sub if sub % 4 in (0, 3) else 8 + (sub - 2) % 8)
            face, k = (4 if node % 4 == 3 else 5), node // 4
        right[16 * face + k, row] = 1
    return left, right


def flux_body(mats_ref, left_ref, right_ref, out_ref):
    dot = functools.partial(jnp.dot, preferred_element_type=jnp.float32, precision=HI)
    parts = [dot(mats_ref[f], right_ref[16 * f : 16 * f + 16]) for f in range(6)]
    full = dot(left_ref[...], jnp.concatenate(parts, axis=0))
    high = full.astype(jnp.bfloat16)
    low = (full - high.astype(jnp.float32)).astype(jnp.bfloat16)
    out_ref[...] = jnp.concatenate(
        [jnp.concatenate([high, high], axis=1), jnp.concatenate([low, low], axis=1)], axis=0
    )


def tables_body(flag_ref, own_ref, pair_ref, cross_ref, inv_near_ref, mass_ref, index_ref, face_ref, coef_ref):
    row = lax.broadcasted_iota(jnp.int32, (64, 128), 0)
    along_b = row < 32
    second = jnp.where(along_b, (row >> 2) & 1, 1 - (row & 1)) == 1
    even = flag_ref[10:11] == 1

    def beside(begin, end):
        pair, cross = pair_ref[begin:end], cross_ref[begin:end]
        return jnp.where(even, cross, pair), jnp.where(even, pair, cross)

    for i in range(8):
        low, high = beside(64 * i, 64 * i + 64)
        inv_near_ref[i], inv_near_ref[8 + i] = merge(low, high), merge_far(low, high)
    low, high = beside(512, 592)
    tiles = [own_ref[0:80, 0:128], own_ref[0:80, 128:256], merge(low, high), merge_far(low, high)]
    for m, tile in enumerate(tiles):
        index = tile[70:74].astype(jnp.int32)
        if m == 3:
            index = (index + 64) & 127

        def spread(rows):
            return jnp.where(along_b, jnp.where(second, rows[1:2], rows[0:1]), jnp.where(second, rows[3:4], rows[2:3]))

        mass_ref[m] = tile[0:64]
        coef_ref[m] = tile[64:72]
        index_ref[m] = spread(index)
        face_ref[m] = spread(tile[66:70])


def sort_terms_body(flag_ref, own_ref, other_ref, out_ref):
    for j in range(8):
        slot = flag_ref[j]

        @pl.when(slot < 4)
        def _():
            out_ref[j] = own_ref[slot & 3]

        @pl.when(slot >= 4)
        def _():
            out_ref[j] = other_ref[slot & 3]


def join_halo_body(*refs):
    out_ref = refs[-1]
    out_ref[0] = refs[0][...]
    out_ref[1] = refs[1][...]


def halo_body(flag_ref, own_ref, other_ref, near_ref, full_ref, far_ref):
    core_0, even = flag_ref[9:10] == 1, flag_ref[10:11] == 1
    first = first_half((4, 64, 128))
    for part in range(2):
        for i in range(0, 20, 4):
            rows = slice(i, i + 4)
            mine, others = (own_ref[0, rows], own_ref[1, rows]), (other_ref[0, rows], other_ref[1, rows])
            yes, no = (mine, others) if part == 0 else (others, mine)
            pair, cross = jnp.where(core_0, yes[0], no[0]), jnp.where(core_0, yes[1], no[1])
            low, high = jnp.where(even, cross, pair), jnp.where(even, pair, cross)
            at = 20 * part + i
            a, b = merge(low, high), merge_far(low, high)
            if at < 32:
                full_ref[at : at + 4], full_ref[32 + at : 36 + at] = a, b
            else:
                far_ref[at - 32 : at - 28], far_ref[at - 24 : at - 20] = a, b
    for i in range(0, 16, 4):
        near_ref[i : i + 4] = jnp.where(first, full_ref[i : i + 4], full_ref[48 + i : 52 + i])


def per_device(
    states, initial, source, mass, inv_fine, inv_coarse, face_mats, face_coef, neighbours, rims
):
    flags, spread = flag_rows()
    pair = f32(2, 64, 128)

    def from_hbm(body, out_shapes, held, inputs, copies, cost):
        hbm = pl.BlockSpec(memory_space=pltpu.HBM)
        scratch = [pltpu.VMEM(a.shape, a.dtype) for a in inputs] + [pltpu.SemaphoreType.DMA((copies,))]
        return call(
            body, out_shapes, *held, *(pltpu.with_memory_space_constraint(a, pltpu.HBM) for a in inputs),
            specs=[VM] * len(held) + [hbm] * len(inputs), scratch=scratch, mib=20, cost=cost,
        )

    cost = pl.CostEstimate(flops=4 << 30, bytes_accessed=16 << 20, transcendentals=0)
    order_row, beside, inv_c, coarse_pair, coarse_cross = from_hbm(
        coarse_body,
        [
            jax.ShapeDtypeStruct((1, 256), jnp.int32), f32(4, 256), vmem_f32(64, 64, 256),
            f32(20, 64, 128), f32(20, 64, 128),
        ],
        [spread], (neighbours, rims, inv_coarse), 10, cost,
    )
    got_coarse = send(coarse_pair, HALO_PAIR), send(coarse_cross, HALO_CROSS)
    start, first_value, src, table, up_start, down_start, inv_f, fine_pair, fine_cross = from_hbm(
        start_body,
        [
            pair, pair, f32(4, 2, 64, 128), f32(80, 256), f32(96, 128), f32(96, 128), vmem_f32(64, 64, 256),
            f32(592, 128), f32(592, 128),
        ],
        [spread, order_row, beside], (states, initial, source, mass, face_coef, inv_fine), 13, cost,
    )
    got_coarse_pair, got_coarse_cross = got_coarse
    up_start, down_start, fine_pair, fine_cross, start, got_coarse_pair = lax.optimization_barrier(
        (up_start, down_start, fine_pair, fine_cross, start, got_coarse_pair)
    )
    low_start, high_start = send(up_start, UP), send(down_start, DOWN)
    got_pair, got_cross = send(fine_pair, HALO_PAIR), send(fine_cross, HALO_CROSS)
    far_start = send(start, FIRST_TO_LAST)
    low_start, high_start, got_pair, got_cross, far_start, got_coarse_cross = lax.optimization_barrier(
        (low_start, high_start, got_pair, got_cross, far_start, got_coarse_cross)
    )
    got_coarse = got_coarse_pair, got_coarse_cross
    fine_near, *tables = call(
        tables_body,
        [
            vmem_f32(16, 64, 128), f32(4, 64, 128), jax.ShapeDtypeStruct((4, 64, 128), jnp.int32), f32(4, 64, 128),
            f32(4, 8, 128),
        ],
        spread, table, got_pair, got_cross,
    )
    left, right = flux_constants()
    mat = call(
        flux_body, [jax.ShapeDtypeStruct((128, 192), jnp.bfloat16)], face_mats, jnp.asarray(left), jnp.asarray(right)
    )[0]

    def fine_march(field, low, high, at, count, other=(), middle=False):
        operands = (
            spread, field, low, high, *tables, mat, pinned(inv_f), fine_near, src[at : at + count],
            low_start, high_start, *other,
        )
        return call(
            functools.partial(fine_body, count, 64 + 8 * at, bool(other), middle), [pair] * (2 if middle else 1),
            *operands,
        )

    def exchange(field):
        return send(field[1], UP), send(field[0], DOWN)

    (field,) = fine_march(start, low_start, high_start, 0, 2)
    low, high = exchange(field)
    (handed,) = fine_march(field, low, high, 2, 2)
    arrived, low, high = send(handed, SLICE), send(handed[1], SLICE_UP), send(handed[0], SLICE_DOWN)

    field, begin = fine_march(arrived, low, high, 0, 2, (start,), middle=True)
    low, high = exchange(field)
    (field,) = fine_march(field, low, high, 2, 2)
    next_term = call(term_body, [pair], spread, field, handed, first_value, far_start)[0]

    joined = call(join_halo_body, [f32(2, 20, 64, 128)], *got_coarse)[0]
    inv_near, inv_full, inv_far = call(
        halo_body, [vmem_f32(16, 64, 128), vmem_f32(64, 64, 128), vmem_f32(16, 64, 128)],
        spread, joined, send(joined, CORE),
    )
    packed = call(pack_terms_body, [f32(208, 128)], next_term, *exchange(next_term))[0]
    terms = call(stack_body, [f32(4, 208, 128)], *(send(packed, pairs) for pairs in GROUP))[0]
    terms = call(sort_terms_body, [f32(8, 208, 128)], flags, terms, send(terms, CORE), specs=[SM, VM, VM])[0]

    value, up, down = next_term, low_start, high_start
    picked = []
    for turn in range(4):
        last = turn == 3
        for at, count in ((0, 3), (3, 3), (6, 2)):
            if at > 0:
                low, high = send(up, UP), send(down, DOWN)
            elif turn > 0:
                value, low, high = send(value, YNEXT), send(up, Y_UP), send(down, Y_DOWN)
            else:
                low, high = up, down
            value, up, down, *picked = call(
                functools.partial(window_body, count, at, at == 0, 0 if turn == 0 else 1, last),
                [pair, f32(80, 128), f32(80, 128)] + [f32(4, 64, 128)] * last,
                spread, value, low, high, *tables, mat,
                pinned(inv_c), pinned(inv_full), pinned(inv_near), pinned(inv_far), pinned(terms),
                *([begin] * last), *picked, scratch=[pltpu.VMEM((3, 64, 128), jnp.float32)],
            )
    kept = picked[0]

    corrected = kept[0:2]
    low, high = exchange(corrected)
    field, middle = fine_march(corrected, low, high, 0, 2, middle=True)
    low, high = exchange(field)
    c_points, residual, others = call(
        restore_body, [f32(1, 64, 256), f32(1, 64, 256), f32(2, 64, 256)],
        order_row, corrected, middle, field, kept[2:4], cost=cost,
    )
    low, high, others = lax.optimization_barrier((low, high, others))
    (final,) = fine_march(field, low, high, 2, 1)
    f_points = call(restore_last_body, [f32(3, 64, 256)], order_row, final, others)[0]
    return c_points, f_points, residual


def solution(mesh):
    return jax.shard_map(
        per_device,
        mesh=mesh,
        in_specs=(
            P("tm", None, "space"),
            P(None, "space"),
            P("tm", None, "space"),
            P(None, "space"),
            P(None, None, "space"),
            P(None, None, "space"),
            P(),
            P(None, "space"),
            P(None, "space"),
            P(None, "space"),
        ),
        out_specs=(P("tm", None, "space"), P("tm", None, "space"), P("tm", None, "space")),
        check_vma=False,
    )
```
